128 devices in a mesh: seq: 2 (over z_lo), dp: 64 (over y, x, z_hi, core).
Axes of the slice: x: 4, y: 4, z: 4 (z_hi: 2, z_lo: 2; z = z_hi * 2 + z_lo), core: 2. Of those that a mesh axis runs over, the one named last changes fastest.
Arguments:
- layer_input: bfloat16 [64, 512, 1024], P('dp', 'seq'), may hold values from -6 to 6
- segments: int32 [64, 512], P('dp', 'seq'), may hold values from 0 to 1, as said below
- positions: int32 [64, 512], P('dp', 'seq'), may hold values from 0 to 2558, as said below
- qkv_weight: bfloat16 [1024, 4096], P(None, ('seq', 'dp')), may hold values from -0.1875 to 0.1875
- out_weight: bfloat16 [2048, 1024], P(('seq', 'dp')), may hold values from -1 to 1
- mlp_weight: bfloat16 [3072, 3, 1024], P(('seq', 'dp')), may hold values from -0.1875 to 0.1875
- gains: bfloat16 [2304], P(('seq', 'dp')), may hold values from 0.25 to 1.75
- cotangent: bfloat16 [64, 512, 1024], P('dp', 'seq'), may hold values from -6 to 6
Outputs:
- layer_output: bfloat16 [64, 512, 1024], P('dp', 'seq')
- input_grad: bfloat16 [64, 512, 1024], P('dp', 'seq')
- qkv_grad: float32 [1024, 4096], P(None, ('seq', 'dp'))
- out_grad: float32 [2048, 1024], P(('seq', 'dp'))
- mlp_grad: float32 [3072, 3, 1024], P(('seq', 'dp'))
- gains_grad: float32 [2304], P(('seq', 'dp'))
The draws below stay inside these ranges and needn't reach their ends.
Inputs may be any that keep to these rules, and one draw needn't show every extreme that they name: `segments`: each sequence holds two documents, numbered 0 then 1, each of 128 tokens or more. Within a document positions rise by one from token to token.
All inputs are finite; a program needn't handle non-finite values.
Results may differ from the reference program's by a relative error of at most 0.018.
Values may be sent and summed in bfloat16 or wider, within the bound.
A program may use at most 256 MiB of HBM per device.

```python
import math
import jax
import jax.numpy as jnp
from jax import lax

D = 1024
FF = 3072
HEADS = 16
KV_HEADS = 8
HEAD = 128
TOK_DEV = 256
SEQS = 64
SEQ_LEN = 512
DOC_MIN = 128
HQ = 2048
QKV = 4096
GAINS = 2304


def doc_layout(key):
    bound_key = jax.random.fold_in(key, 5)
    boundary = jax.random.randint(bound_key, (SEQS, 1), DOC_MIN, SEQ_LEN - DOC_MIN).astype(jnp.int32)
    boundary = boundary + (boundary >= TOK_DEV).astype(jnp.int32)
    token_order = jnp.arange(SEQ_LEN, dtype=jnp.int32)[None, :]
    segment = (token_order >= boundary).astype(jnp.int32)
    return (boundary, token_order, segment)


def draw_segments(key, part):
    layout = doc_layout(key)
    return layout[2].astype(jnp.int32)


def draw_positions(key, part):
    boundary, token_order, segment = doc_layout(key)
    doc_start = segment * boundary
    doc_offset = segment * (boundary + 2047)
    return (doc_offset + token_order - doc_start).astype(jnp.int32)


def levels(key, dims, cuts, smallest, top_value):
    loudness, own = 1.0, jax.random.fold_in(key, 6)
    for dim, blocks in cuts:
        heights = jnp.exp(jax.random.uniform(jax.random.fold_in(own, dim), (blocks,), jnp.float32, smallest / len(cuts), top_value / len(cuts)))
        loudness = loudness * jnp.repeat(heights, dims[dim] // blocks).reshape([-1 if axis == dim else 1 for axis in range(len(dims))])
    return loudness


def normal_values(key, shape, deviation, most, pieces=(), kind=jnp.bfloat16):
    drawn = deviation * jax.random.normal(key, shape, jnp.float32)
    if pieces:
        drawn = drawn * levels(key, shape, pieces, -0.22, 0.18)
    return jnp.clip(drawn, -most, most).astype(kind)


def setup_inputs(seed: int = 0) -> dict:
    splits = jax.random.split(jax.random.key(seed), 9)
    return {
        "layer_input": normal_values(splits[0], (SEQS, SEQ_LEN, D), 1.0, 6.0, ((0, 64), (1, 2))),
        "segments": draw_segments(jax.random.fold_in(splits[8], 71), 0),
        "positions": draw_positions(jax.random.fold_in(splits[8], 71), 0),
        "qkv_weight": normal_values(splits[3], (D, QKV), D ** -0.5, 0.1875, ((1, 128),)),
        "out_weight": normal_values(splits[4], (HQ, D), (HQ // 64) ** -0.5, 1.0, ((0, 128),)),
        "mlp_weight": normal_values(splits[5], (FF, 3, D), D ** -0.5, 0.1875, ((0, 128),)),
        "gains": jnp.clip(1.0 + 0.15 * jax.random.normal(splits[6], (GAINS,), jnp.float32), 0.25, 1.75).astype(jnp.bfloat16),
        "cotangent": normal_values(splits[7], (SEQS, SEQ_LEN, D), 1.0, 6.0, ((0, 64), (1, 2))),
    }


EPSILON = 1e-06
THETA_BASE = 1000000.0
MASKED = -1e+30

@jax.custom_vjp
def low(v):
    return lax.optimization_barrier(v.astype(jnp.bfloat16)).astype(jnp.float32)

@jax.custom_vjp
def low_back(v):
    return v

def low_keep(v):
    return (low(v), None)

def low_pass(kept, grad):
    return (grad,)

def back_keep(v):
    return (v, None)

def back_low(kept, grad):
    return (low(grad),)
low.defvjp(low_keep, low_pass)
low_back.defvjp(back_keep, back_low)

def matmul(left, right):
    return jnp.dot(left, right, precision=lax.Precision.HIGHEST)

def rms_norm(values, gain):
    return values * lax.rsqrt(lax.optimization_barrier(jnp.mean(values * values, axis=-1, keepdims=True)) + EPSILON) * gain

def rope_tables(places):
    half_size = HEAD // 2
    freqs = THETA_BASE ** (-(jnp.arange(half_size, dtype=jnp.float32) * 2.0) / HEAD)
    angles = places.astype(jnp.float32)[..., None] * freqs
    cosine = jnp.concatenate([jnp.cos(angles), jnp.cos(angles)], axis=-1)[..., None, :]
    sine = jnp.concatenate([jnp.sin(angles), jnp.sin(angles)], axis=-1)[..., None, :]
    return (cosine, sine)

def rotate(values, cosine, sine):
    first_half, second_half = jnp.split(values, 2, axis=-1)
    return values * cosine + jnp.concatenate([-second_half, first_half], axis=-1) * sine

def attend(item):
    queries, keys, values, segment = item
    length = segment.shape[0]
    grouped = queries.reshape(length, KV_HEADS, HEADS // KV_HEADS, HEAD)
    scores = jnp.einsum('tkgd,ukd->kgtu', grouped, keys, precision=lax.Precision.HIGHEST) * HEAD ** (-0.5)
    scores = low_back(scores)
    order = jnp.arange(length, dtype=jnp.int32)
    allowed = (segment[:, None] == segment[None, :]) & (order[None, :] <= order[:, None])
    scores = jnp.where(allowed[None, None], scores, MASKED)
    exponent = jnp.exp(scores - lax.optimization_barrier(jnp.max(scores, axis=-1, keepdims=True)))
    weights_low = low(exponent / lax.optimization_barrier(jnp.sum(exponent, axis=-1, keepdims=True)))
    context = jnp.einsum('kgtu,ukd->tkgd', weights_low, values, precision=lax.Precision.HIGHEST)
    return context.reshape(length, HEADS * HEAD)

def layer(inputs, segment, places, params):
    w_qkv, w_out, w_mlp, gain_full = params
    group_seqs = inputs.shape[0]
    row_count = group_seqs * SEQ_LEN
    query_width = HEADS * HEAD
    key_width = KV_HEADS * HEAD
    gain_in = gain_full[:D]
    gain_mlp = gain_full[D:2 * D]
    gain_query = gain_full[2 * D:2 * D + HEAD]
    gain_key = gain_full[2 * D + HEAD:]
    input_normed = low(rms_norm(inputs, gain_in))
    projected = low_back(matmul(input_normed.reshape(row_count, D), w_qkv))
    projected = projected.reshape(group_seqs, SEQ_LEN, query_width + 2 * key_width)
    query_pre = projected[..., :query_width].reshape(group_seqs, SEQ_LEN, HEADS, HEAD)
    key_pre = projected[..., query_width:query_width + key_width].reshape(group_seqs, SEQ_LEN, KV_HEADS, HEAD)
    value_pre = projected[..., query_width + key_width:].reshape(group_seqs, SEQ_LEN, KV_HEADS, HEAD)
    cosine, sine = rope_tables(places)
    queries = low(rotate(rms_norm(query_pre, gain_query), cosine, sine))
    keys = low(rotate(rms_norm(key_pre, gain_key), cosine, sine))
    values = low(value_pre)
    context = lax.map(jax.checkpoint(attend), (queries, keys, values, segment))
    context = low(low_back(context)).reshape(row_count, query_width)
    hidden_res = inputs.reshape(row_count, D) + low_back(matmul(context, w_out))
    mlp_in = low(rms_norm(hidden_res, gain_mlp))
    gate_pre = low_back(matmul(mlp_in, w_mlp[:, 0, :].T))
    up_pre = low_back(matmul(mlp_in, w_mlp[:, 1, :].T))
    activated = low(gate_pre * jax.nn.sigmoid(gate_pre) * up_pre)
    mlp_out = low_back(matmul(activated, w_mlp[:, 2, :]))
    return (hidden_res + mlp_out).reshape(inputs.shape)

def reference(layer_input, segments, positions, qkv_weight, out_weight, mlp_weight, gains, cotangent):
    group_seqs = math.gcd(SEQS, max(1, 4096 // SEQ_LEN))
    group_count = SEQS // group_seqs
    params = (qkv_weight.astype(jnp.float32), out_weight.astype(jnp.float32), mlp_weight.astype(jnp.float32), gains.astype(jnp.float32))

    def split_groups(array):
        return array.reshape((group_count, group_seqs) + array.shape[1:])

    def one_group(totals, item):
        inputs, segment, places, incoming = item

        def forward(values, weights):
            return layer(values, segment, places, weights)
        result, pull_back = jax.vjp(forward, inputs.astype(jnp.float32), params)
        input_grad, weight_grads = pull_back(incoming.astype(jnp.float32))
        totals = jax.tree.map(jnp.add, totals, weight_grads)
        return (totals, (result.astype(jnp.bfloat16), input_grad.astype(jnp.bfloat16)))
    initial = jax.tree.map(jnp.zeros_like, params)
    totals, (outputs, input_grads) = lax.scan(one_group, initial, (split_groups(layer_input), split_groups(segments), split_groups(positions), split_groups(cotangent)))
    return (outputs.reshape(layer_input.shape), input_grads.reshape(layer_input.shape), totals[0], totals[1], totals[2], totals[3])
```

```python
import functools
import jax, jax.numpy as jnp
from jax import lax
from jax.experimental import pallas as pl
from jax.experimental.pallas import tpu as pltpu
from jax.sharding import PartitionSpec as P

MESH = pl.DeviceIdType.MESH
BF = jnp.bfloat16
F32 = jnp.float32
LQ = 256
HEAD = 128
EPSILON = 1e-06
THETA_BASE = 1000000.0
MASKED = -1e30
VMEM_BYTES = 63 << 20
SHAPES = {"q": (4, 2, 2, 2, 32, 1024), "k": (4, 2, 2, 2, 32, 1024), "o": (2, 2, 4, 2, 2, 16, 1024),
          "g": (4, 4, 2, 48, 1024), "u": (4, 4, 2, 48, 1024), "d": (4, 4, 2, 48, 1024)}
ORDERS = {"q": "xyz", "k": "yzx", "o": "zxy", "g": "xyz", "u": "yzx", "d": "zxy"}
KINDS = "qkogud"


def pick(kind, x, y, z, h):
    every = slice(None)
    at = lambda v: every if v is None else v
    low = lambda v: every if v is None else v % 2
    high = lambda v: every if v is None else v // 2
    lanes = every if z is None else pl.ds(pl.multiple_of(z * LQ, LQ), LQ)
    if kind == "q":
        return (at(y), low(x), at(h), high(x), every, lanes)
    if kind == "k":
        return (at(y), high(x), at(h), low(x), every, lanes)
    if kind == "o":
        return (at(h), high(y), at(x), every, low(y), every, lanes)
    return (at(x), at(y), at(h), every, lanes)


def half_shape(kind, full, axis):
    n = lambda a: 4 if a in full else None
    x, y, z = n("x"), n("y"), n("z")
    lanes = 1024 if z else 256
    if kind in "qk":
        s = ([4] if y else []) + ([2, 2] if x else []) + [32, lanes]
    elif kind == "o":
        s = ([2] if y else []) + ([4] if x else []) + [2] + ([2] if y else []) + [16, lanes]
    else:
        s = ([4] if x else []) + ([4] if y else []) + [48, lanes]
    return tuple(s)


class Place:
    def __init__(self):
        s, d = lax.axis_index("seq"), lax.axis_index("dp")
        self.zlo = s
        self.core = d % 2
        self.zhi = (d // 2) % 2
        self.x = (d // 4) % 4
        self.y = d // 16
        self.z = self.zhi * 2 + s

    def dev(self, x=None, y=None, z=None, core=None):
        x = self.x if x is None else x
        y = self.y if y is None else y
        z = self.z if z is None else z
        core = self.core if core is None else core
        return (z % 2, ((y * 4 + x) * 2 + z // 2) * 2 + core)

    def at(self, axis):
        return {"x": self.x, "y": self.y, "z": self.z}[axis]

    def ring(self, axis, step):
        return self.dev(**{axis: (self.at(axis) + step) % 4})


def flip(v):
    return v + 1 - 2 * (v % 2)


def region(me, kind, full, axis, val, h=None):
    c = {a: (None if a in full else me.at(a)) for a in "xyz"}
    c[axis] = val
    return pick(kind, c["x"], c["y"], c["z"], h)


def remote(src, dst, send, recv, device):
    return pltpu.make_async_remote_copy(src_ref=src, dst_ref=dst, send_sem=send, recv_sem=recv, device_id=device, device_id_type=MESH)


class Gather:
    def __init__(self, me, kind, phase, buf, send, recv, base):
        self.me, self.kind, self.buf, self.send, self.recv, self.base = me, kind, buf, send, recv, base
        order = ORDERS[kind]
        self.axis, self.full = order[phase], order[:phase]

    def reg(self, step, h=None):
        return self.buf.at[region(self.me, self.kind, self.full, self.axis, (self.me.at(self.axis) + step + 4) % 4, h)]

    def copy(self, n, step, h, hop):
        r = self.reg(step, h)
        return remote(r, r, self.send.at[self.base + n], self.recv.at[self.base + n], self.me.ring(self.axis, hop % 4))

    def start(self):
        self.copy(0, 0, None, 1).start()
        self.copy(1, 0, None, -1).start()

    def forward(self):
        self.copy(0, -1, None, 1).wait_recv()
        self.copy(2, -1, 0, 1).start()
        self.copy(1, 1, None, -1).wait_recv()
        self.copy(3, 1, 1, -1).start()

    def finish(self):
        self.copy(2, -2, 0, 1).wait_recv()
        self.copy(3, 2, 1, -1).wait_recv()

    def drain(self):
        self.copy(0, 0, None, 1).wait_send()
        self.copy(1, 0, None, -1).wait_send()
        self.copy(2, -1, 0, 1).wait_send()
        self.copy(3, 1, 1, -1).wait_send()


class Scatter:
    def __init__(self, me, kind, phase, buf, land, send, recv, base, final=None):
        self.me, self.kind, self.buf, self.land, self.send, self.recv, self.base = me, kind, buf, land, send, recv, base
        order = ORDERS[kind]
        self.axis, self.full = order[phase], order[:phase]
        self.final = final

    def idx(self, step, h):
        return region(self.me, self.kind, self.full, self.axis, (self.me.at(self.axis) + step + 4) % 4, h)

    def copy(self, n, src, hop):
        return remote(src, self.land.at[n], self.send.at[self.base + n], self.recv.at[self.base + n], self.me.ring(self.axis, hop % 4))

    def raw(self, n):
        step, h, hop = {4: (2, 0, 1), 5: (2, 1, -1), 1: (1, 1, 1), 3: (-1, 0, -1)}[n]
        return self.copy(n, self.buf.at[self.idx(step, h)], hop)

    def start(self):
        for n in (4, 5, 1, 3):
            self.raw(n).start()

    def forward(self):
        for n, step, h, to, hop in ((4, 1, 0, 0, 1), (5, -1, 1, 2, -1)):
            self.raw(n).wait_recv()
            total = self.land[n].astype(F32) + self.buf[self.idx(step, h)].astype(F32)
            self.land[n] = total.astype(BF)
            self.copy(to, self.land.at[n], hop).start()

    def finish(self):
        self.copy(0, self.land.at[4], 1).wait_recv()
        self.raw(3).wait_recv()
        self.raw(1).wait_recv()
        self.copy(2, self.land.at[5], -1).wait_recv()
        for h, a, b in ((0, 0, 3), (1, 2, 1)):
            total = self.land[a].astype(F32) + self.land[b].astype(F32) + self.buf[self.idx(0, h)].astype(F32)
            if self.final is None:
                self.buf[self.idx(0, h)] = total.astype(BF)
            else:
                self.final[h] = total

    def drain(self):
        for n in (4, 5, 1, 3):
            self.raw(n).wait_send()
        self.copy(0, self.land.at[4], 1).wait_send()
        self.copy(2, self.land.at[5], -1).wait_send()


def greet(me):
    bar = pltpu.get_barrier_semaphore()
    x, y, z, c = me.x, me.y, me.z, me.core
    friends = [me.ring("x", s) for s in (1, 2, 3)] + [me.ring("y", s) for s in (1, 2, 3)] + [me.ring("z", s) for s in (1, 2, 3)]
    friends.append(me.dev(core=1 - c))
    for s in range(4):
        zz = (z + s) % 4
        friends.append(me.dev(x=(x + 2) % 4, z=zz, core=1 - c))
        friends.append(me.dev(x=flip(x), z=zz, core=1 - c))
        friends.append(me.dev(y=flip(y), z=zz, core=1 - c))
    friends.append(me.dev(z=flip(z), core=1 - c))
    for f in friends:
        pl.semaphore_signal(bar, inc=1, device_id=f, device_id_type=MESH)
    pl.semaphore_wait(bar, len(friends))


class Route:
    def __init__(self, own, src, dst, send, recv, local, device):
        self.own = own
        self.made_far = lambda: remote(src, dst, send, recv, device)
        self.made_near = lambda: pltpu.make_async_copy(src, dst, local)

    def start(self):
        if self.own is None:
            self.made_far().start()
        else:
            pl.when(self.own)(lambda: self.made_near().start())
            pl.when(jnp.logical_not(self.own))(lambda: self.made_far().start())

    def wait_recv(self):
        if self.own is None:
            self.made_far().wait_recv()
        else:
            pl.when(self.own)(lambda: self.made_near().wait())
            pl.when(jnp.logical_not(self.own))(lambda: self.made_far().wait_recv())

    def wait_send(self):
        if self.own is None:
            self.made_far().wait_send()
        else:
            pl.when(jnp.logical_not(self.own))(lambda: self.made_far().wait_send())


def mapping(me, kind):
    x, y, c = me.x, me.y, me.core
    if kind == "q":
        own = (c + x // 2 + 1) % 2
        return own, dict(x=(x + 2 * (1 - own)) % 4, y=y, core=(c + 1 - own) % 2)
    if kind == "k":
        own = (c + x + 1) % 2
        return own, dict(x=x + (1 - own) * (1 - 2 * (x % 2)), y=y, core=(c + 1 - own) % 2)
    own = (c + y + 1) % 2
    return own, dict(x=x, y=y + (1 - own) * (1 - 2 * (y % 2)), core=(c + 1 - own) % 2)


def lanes_of(z):
    return pl.ds(pl.multiple_of(z * LQ, LQ), LQ)


class Spread:
    def __init__(self, me, wq, wo, wm, bufs, stage, send, recv, local):
        self.me, self.wq, self.wo, self.wm, self.bufs, self.stage = me, wq, wo, wm, bufs, stage
        self.send, self.recv, self.local = send, recv, local

    def qk(self, kind, dz, zsrc, to=None):
        me = self.me
        own, col = mapping(me, kind)
        z = (me.z + dz) % 4
        place = dict(x=me.x, y=me.y) if to is None else col
        dst = self.bufs[kind].at[pick_piece(kind, place["x"], place["y"], z, zsrc)]
        n = zsrc // 2
        return Route((own == 1) & (zsrc == z), self.wq.at[:, lanes_of(z)], dst, self.send.at[dz],
                     self.recv.at[(0 if kind == "q" else 2) + n], self.local.at[0], me.dev(z=z, **col))

    def o(self, dz, zsrc, place):
        me = self.me
        own, col = mapping(me, "o")
        z = (me.z + dz) % 4
        y = me.y if place is None else col["y"]
        dst = self.bufs["o"].at[zsrc % 2, y // 2, me.x, zsrc // 2, y % 2, slice(None), lanes_of(z)]
        return Route((own == 1) & (zsrc == z), self.wo.at[:, lanes_of(z)], dst, self.send.at[4 + dz],
                     self.recv.at[4 + zsrc], self.local.at[1], me.dev(z=z, **col))

    def m(self, dz):
        me = self.me
        z = (me.z + dz) % 4
        return remote(self.wm.at[:, lanes_of(z)], self.stage.at[dz], self.send.at[8 + dz], self.recv.at[8 + dz], me.dev(z=z))

    def start_attention(self):
        me = self.me
        for kind, low in (("q", 0), ("k", 1)):
            @pl.when(me.zlo == low)
            def _(kind=kind):
                for dz in range(4):
                    self.qk(kind, dz, me.z, to=1).start()
        for dz in range(4):
            self.o(dz, me.z, 1).start()

    def start_mlp(self):
        for dz in range(1, 4):
            self.m(dz).start()

    def wait_attention(self):
        for n in range(2):
            self.qk("q", 0, 2 * n).wait_recv()
            self.qk("k", 0, 2 * n + 1).wait_recv()
        for zs in range(4):
            self.o(0, zs, None).wait_recv()

    def wait_mlp(self):
        me = self.me
        for dz in range(1, 4):
            self.m(dz).wait_recv()
        self.stage[0] = self.wm[:, lanes_of(me.z)]
        for t, kind in enumerate("gud"):
            rows = [self.stage[(me.z - zs + 4) % 4, t * 24:(t + 1) * 24, :] for zs in range(4)]
            block = jnp.concatenate(rows, axis=0).astype(BF)
            for h in range(2):
                self.bufs[kind][me.x, me.y, h, :, lanes_of(me.z)] = block[h * 48:(h + 1) * 48]

    def drain(self):
        me = self.me
        for kind, low in (("q", 0), ("k", 1)):
            @pl.when(me.zlo == low)
            def _(kind=kind):
                for dz in range(4):
                    self.qk(kind, dz, me.z, to=1).wait_send()
        for dz in range(4):
            self.o(dz, me.z, 1).wait_send()
        for dz in range(1, 4):
            self.m(dz).wait_send()


def pick_piece(kind, x, y, z, zsrc):
    every = slice(None)
    if kind == "q":
        return (y, x % 2, zsrc // 2, x // 2, every, lanes_of(z))
    return (y, x // 2, zsrc // 2, x % 2, every, lanes_of(z))


class Collect:
    def __init__(self, me, oq, oo, om, finals, send, recv, local):
        self.me, self.oq, self.oo, self.om, self.finals = me, oq, oo, om, finals
        self.send, self.recv, self.local = send, recv, local

    def qk(self, kind, dz):
        me = self.me
        own, col = mapping(me, kind)
        z = (me.z + dz) % 4
        keep = (own == 1) if dz == 0 else None
        return Route(keep, self.finals[kind].at[z // 2], self.oq.at[:, lanes_of(me.z)], self.send.at[dz],
                     self.recv.at[dz], self.local.at[0], me.dev(z=z, **col))

    def o(self, dz):
        me = self.me
        own, col = mapping(me, "o")
        z = (me.z + dz) % 4
        keep = (own == 1) if dz == 0 else None
        return Route(keep, self.finals["o"].at[z % 2, z // 2], self.oo.at[:, lanes_of(me.z)], self.send.at[4 + dz],
                     self.recv.at[4 + dz], self.local.at[1], me.dev(z=z, **col))

    def m(self, t, kind, dz):
        me = self.me
        z = (me.z + dz) % 4
        n = 8 + 4 * t + dz
        src = self.finals[kind].at[z // 2, pl.ds(pl.multiple_of((z % 2) * 24, 8), 24)]
        dst = self.om.at[pl.ds(t * 24, 24), lanes_of(me.z)]
        if dz == 0:
            return pltpu.make_async_copy(src, dst, self.local.at[2 + t])
        return remote(src, dst, self.send.at[n], self.recv.at[n], me.dev(z=z))

    def each_qk(self, act):
        me = self.me
        for dz in range(4):
            for kind, low in (("q", 0), ("k", 1)):
                @pl.when((me.z + dz) % 2 == low)
                def _(kind=kind, dz=dz):
                    act(self.qk(kind, dz))

    def start(self, kind):
        if kind == "qk":
            self.each_qk(lambda r: r.start())
        elif kind == "o":
            for dz in range(4):
                self.o(dz).start()
        else:
            for dz in range(4):
                self.m("gud".index(kind), kind, dz).start()

    def finish(self, kind):
        me = self.me
        if kind == "qk":
            for dz in range(4):
                for k, low in (("q", 0), ("k", 1)):
                    @pl.when(me.zlo == low)
                    def _(k=k, dz=dz):
                        self.qk(k, dz).wait_recv()
            self.each_qk(lambda r: r.wait_send())
        elif kind == "o":
            for dz in range(4):
                self.o(dz).wait_recv()
                self.o(dz).wait_send()
        else:
            for dz in range(4):
                c = self.m("gud".index(kind), kind, dz)
                if dz == 0:
                    c.wait()
                else:
                    c.wait_recv()
                    c.wait_send()


def dot(a, b):
    return jnp.dot(a, b, preferred_element_type=F32)


def dot_t(a, b):
    return lax.dot_general(a, b, (((1,), (1,)), ((), ())), preferred_element_type=F32)


def dot_c(a, b):
    return lax.dot_general(a, b, (((0,), (0,)), ((), ())), preferred_element_type=F32)


def mean_last(v):
    return jnp.mean(v, axis=-1, keepdims=True)


def norm_scale(v):
    return lax.rsqrt(mean_last(v * v) + EPSILON)


def norm_back(dz, v, gain):
    r = norm_scale(v)
    n = v * r
    w = dz * gain
    return r * (w - n * mean_last(w * n)), dz * n


def fold_rows(v):
    return jnp.sum(v.reshape(v.shape[0] // 8, 8, v.shape[1]), axis=0)


def rows_of(i, n):
    return pl.ds(pl.multiple_of(i * n, n), n)


class SmallSum:
    def __init__(self, me, buf, land, send, recv):
        self.me, self.buf, self.land, self.send, self.recv = me, buf, land, send, recv

    def copies(self, stage):
        if stage == 0:
            return [remote(self.buf, self.land.at[0], self.send.at[0], self.recv.at[0], self.me.dev(core=1 - self.me.core))]
        first = 1 + 3 * (stage - 1)
        return [remote(self.buf, self.land.at[first + s], self.send.at[first + s], self.recv.at[first + s],
                       self.me.ring("xyz"[stage - 1], s + 1)) for s in range(3)]

    def start(self, stage):
        for c in self.copies(stage):
            c.start()

    def finish(self, stage):
        for c in self.copies(stage):
            c.wait()
        if stage == 0:
            self.buf[...] = self.buf[...] + self.land[0]
        else:
            first = 1 + 3 * (stage - 1)
            self.buf[...] = self.buf[...] + (self.land[first] + self.land[first + 1] + self.land[first + 2])


class Layer:
    def __init__(self, me, S):
        self.me = me
        self.__dict__.update(S)
        c = me.core
        self.mine = rows_of(c, 256)
        self.theirs = rows_of(1 - c, 256)
        self.peer = me.dev(core=1 - c)
        self.wq2 = self.bq.reshape(1024, 1024)
        self.wk2 = self.bk.reshape(1024, 1024)
        self.wo2 = self.bo.reshape(1024, 1024)
        self.wg2 = self.bg.reshape(1536, 1024)
        self.wu2 = self.bu.reshape(1536, 1024)
        self.wd2 = self.bd.reshape(1536, 1024)
        self.dq2 = self.tq.reshape(1024, 1024)
        self.dk2 = self.tk.reshape(1024, 1024)
        self.cx, self.mi = self.dq2.at[pl.ds(0, 512)], self.dq2.at[pl.ds(512, 512)]
        self.es = self.dp.at[:, pl.ds(0, 1024)]
        self.lob, self.igb = self.ct.at[pl.ds(0, 256)], self.ct.at[pl.ds(256, 256)]
        self.da, self.dc = self.dk2.at[pl.ds(0, 512)], self.dk2.at[pl.ds(512, 512)]

    def swap(self, n, src, dst):
        me = self.me
        return Route(me.core == me.zlo, src, dst, self.xsend.at[n], self.xrecv.at[n], self.xlocal.at[n],
                     me.dev(z=me.zhi * 2 + me.core, core=me.zlo))

    def share(self, n, src, dst):
        return remote(src, dst, self.xsend.at[n], self.xrecv.at[n], self.peer)

    def tokens_in(self):
        theirs_there = rows_of(self.me.zlo, 256)
        return [self.swap(0, self.x_in, self.xa.at[theirs_there]),
                self.swap(1, self.meta_in, self.meta.at[self.me.zlo]),
                self.swap(2, self.ct_in, self.ct.at[theirs_there])]

    def tokens_across(self):
        m = self.mine
        return [self.share(3, self.xa.at[m], self.xa.at[m]),
                self.share(4, self.meta.at[self.me.core], self.meta.at[self.me.core]),
                self.share(5, self.ct.at[m], self.ct.at[m])]

    def gains_rows(self):
        for i in range(8):
            cols = slice(i * 128, (i + 1) * 128)
            self.gv[0:1, cols] = self.ga[i:i + 1, :]
            self.gv[1:2, cols] = self.ga[8 + i:9 + i, :]
        self.gv[2:3, 0:128] = self.ga[16:17, :]
        self.gv[2:3, 128:256] = self.ga[17:18, :]

    def tables(self):
        for h in range(2):
            place = jnp.broadcast_to(self.meta[h, 1:2, :].astype(F32), (128, 256)).T
            angle = place * self.consts[0:1, :]
            self.cosine[h * 256:(h + 1) * 256] = jnp.cos(angle)
            self.sine[h * 256:(h + 1) * 256] = jnp.sin(angle) * self.consts[1:2, :]
        for q in range(2):
            seg_q = jnp.broadcast_to(self.meta[q, 0:1, :].astype(F32), (128, 256)).T[:, 0:1]
            for k in range(2):
                seg_k = self.meta[k, 0:1, :].astype(F32)
                row = lax.broadcasted_iota(jnp.int32, (256, 256), 0) + q * 256
                col = lax.broadcasted_iota(jnp.int32, (256, 256), 1) + k * 256
                allowed = (seg_q == seg_k) & (col <= row)
                self.mask[q * 256:(q + 1) * 256, k * 256:(k + 1) * 256] = jnp.where(allowed, 0.0, MASKED).astype(BF)

    def norm_in(self):
        gain = self.gv[0:1, :]

        @pl.loop(0, 8)
        def _(i):
            r = rows_of(i, 64)
            v = self.xa[r].astype(F32)
            self.xn[r] = (v * norm_scale(v) * gain).astype(BF)

    def rope(self, n):
        return n * self.cosine[...] + pltpu.roll(n, 64, 1) * self.sine[...]

    def unrope(self, d, rows):
        return d * self.cosine[rows] - pltpu.roll(d, 64, 1) * self.sine[rows]

    def project(self):
        gq, gk = self.gv[2:3, 0:128], self.gv[2:3, 128:256]

        @pl.loop(0, 4)
        def _(i):
            pre = dot_t(self.xn[...], self.wq2[rows_of(i, 256)])
            for g in range(2):
                v = pre[:, g * 128:(g + 1) * 128]
                cols = pl.ds(pl.multiple_of(i * 256 + g * 128, 128), 128)
                self.qp[:, cols] = v.astype(BF)
                self.qr[:, cols] = self.rope(v * norm_scale(v) * gq).astype(BF)

        @pl.loop(0, 2)
        def _(i):
            pre = dot_t(self.xn[...], self.wk2[rows_of(i, 256)])
            for g in range(2):
                v = pre[:, g * 128:(g + 1) * 128]
                cols = pl.ds(pl.multiple_of(i * 256 + g * 128, 128), 128)
                self.kp[:, cols] = v.astype(BF)
                self.kr[:, cols] = self.rope(v * norm_scale(v) * gk).astype(BF)
            self.vl[:, rows_of(i, 256)] = dot_t(self.xn[...], self.wk2[rows_of(i + 2, 256)]).astype(BF)

    def attend(self):
        factor = HEAD ** -0.5 * 1.4426950408889634

        @pl.loop(0, 4)
        def _(k):
            kcols = rows_of(k, 128)
            for b in range(2):
                n = 256 * (b + 1)
                rows = slice(b * 256, (b + 1) * 256)
                keys, values = self.kr[0:n, kcols], self.vl[0:n, kcols]
                for g in range(2):
                    qcols = pl.ds(pl.multiple_of(k * 256 + g * 128, 128), 128)
                    s = dot_t(self.qr[rows, qcols], keys)
                    p = jnp.exp2(s * factor + self.mask[rows, 0:n].astype(F32))
                    p = (p * (1.0 / jnp.sum(p, axis=-1, keepdims=True))).astype(BF)
                    (self.p0 if b == 0 else self.p1)[2 * k + g] = p
                    self.cx[rows, qcols] = dot(p, values).astype(BF)

    def exchange(self, n, chunk, land):
        cols = slice(chunk * 256, (chunk + 1) * 256)
        return self.share(n + chunk, self.es.at[:, cols], land.at[:, cols])

    def out_project(self):
        for j in range(4):
            cols = slice(j * 256, (j + 1) * 256)
            part = dot(self.cx[...], self.wo2[:, cols])
            self.es[:, cols] = part.astype(BF)
            self.exchange(6, j, self.r0).start()
            self.hid[:, cols] = part + self.xa[:, cols].astype(F32)

    def norm_mid(self):
        for j in range(4):
            self.exchange(6, j, self.r0).wait()
        gain = self.gv[1:2, :]

        @pl.loop(0, 8)
        def _(i):
            r = rows_of(i, 64)
            v = self.hid[r] + self.r0[r].astype(F32)
            self.hid[r] = v
            self.mi[r] = (v * norm_scale(v) * gain).astype(BF)

    def feed_forward(self, c):
        r = rows_of(c, 256)
        gate = dot_t(self.mi[...], self.wg2[r])
        up = dot_t(self.mi[...], self.wu2[r])
        back = dot_t(self.ct[...], self.wd2[r])
        sig = jax.nn.sigmoid(gate)
        silu = gate * sig
        act = (silu * up).astype(BF)
        d_gate = (back * up * sig * (1.0 + gate * (1.0 - sig))).astype(BF)
        d_up = (back * silu).astype(BF)
        self.acc_o[...] += dot(act, self.wd2[r])
        self.acc_d[...] += dot(d_gate, self.wg2[r]) + dot(d_up, self.wu2[r])
        self.wd2[r] = dot_c(act, self.ct[...]).astype(BF)
        self.wg2[r] = dot_c(d_gate, self.mi[...]).astype(BF)
        self.wu2[r] = dot_c(d_up, self.mi[...]).astype(BF)

    def send_mid(self):
        self.es[...] = self.acc_d[...].astype(BF)
        for j in range(4):
            self.exchange(10, j, self.r1).start()

    def norm_mid_back(self):
        for j in range(4):
            self.exchange(10, j, self.r1).wait()
        gain = self.gv[1:2, :]

        def body(i, total):
            r = rows_of(i, 64)
            dz = self.acc_d[r] + self.r1[r].astype(F32)
            dv, term = norm_back(dz, self.hid[r], gain)
            d = self.ct[r].astype(F32) + dv
            self.acc_d[r] = d
            self.da[r] = d.astype(BF)
            return total + fold_rows(term) * (i // 4 == self.me.core).astype(F32)

        total = lax.fori_loop(0, 8, body, jnp.zeros((8, 1024), F32))
        self.gg[1:2, :] = jnp.sum(total, axis=0, keepdims=True)

    def finish_output(self):
        self.ls[...] = self.acc_o[self.theirs].astype(BF)
        self.share(14, self.ls, self.r0.at[pl.ds(0, 256)]).start()
        self.share(14, self.ls, self.r0.at[pl.ds(0, 256)]).wait()
        self.lob[...] = (self.acc_o[self.mine] + self.hid[self.mine] + self.r0[0:256].astype(F32)).astype(BF)
        self.swap(15, self.lob, self.lo).start()

    def out_back(self):
        for j in range(4):
            r = slice(j * 256, (j + 1) * 256)
            self.dc[:, r] = dot_t(self.da[...], self.wo2[r]).astype(BF)
        for j in range(4):
            r = slice(j * 256, (j + 1) * 256)
            self.wo2[r] = dot_c(self.cx[:, r], self.da[...]).astype(BF)

    def attend_back(self):
        scale = HEAD ** -0.5
        gq, gk = self.gv[2:3, 0:128], self.gv[2:3, 128:256]

        def body(k, totals):
            total_q, total_k = totals
            kcols = rows_of(k, 128)
            dk, dv = [0.0, 0.0], [0.0, 0.0]
            for b in range(2):
                n = 256 * (b + 1)
                rows = slice(b * 256, (b + 1) * 256)
                keys, values = self.kr[0:n, kcols], self.vl[0:n, kcols]
                for g in range(2):
                    qcols = pl.ds(pl.multiple_of(k * 256 + g * 128, 128), 128)
                    low = (self.p0 if b == 0 else self.p1)[2 * k + g]
                    dc = self.dc[rows, qcols]
                    p = low.astype(F32)
                    t = p * dot_t(dc, values)
                    ds = (t - p * jnp.sum(t, axis=-1, keepdims=True)).astype(BF)
                    dz = self.unrope(dot(ds, keys) * scale, rows)
                    dq, term = norm_back(dz, self.qp[rows, qcols].astype(F32), gq)
                    self.dp[rows, qcols] = dq.astype(BF)
                    total_q = total_q + fold_rows(term)
                    pk, pv = dot_c(ds, self.qr[rows, qcols]), dot_c(low, dc)
                    for j in range(b + 1):
                        part = slice(j * 256, (j + 1) * 256)
                        dk[j] = dk[j] + pk[part]
                        dv[j] = dv[j] + pv[part]
            for j in range(2):
                rows = slice(j * 256, (j + 1) * 256)
                dz = self.unrope(dk[j] * scale, rows)
                dkey, term = norm_back(dz, self.kp[rows, kcols].astype(F32), gk)
                self.dp[rows, pl.ds(pl.multiple_of(1024 + k * 128, 128), 128)] = dkey.astype(BF)
                self.dp[rows, pl.ds(pl.multiple_of(1536 + k * 128, 128), 128)] = dv[j].astype(BF)
                total_k = total_k + fold_rows(term)
            return total_q, total_k

        zero = jnp.zeros((8, 128), F32)
        total_q, total_k = lax.fori_loop(0, 4, body, (zero, zero))
        self.gg[2:3, 0:128] = jnp.sum(total_q, axis=0, keepdims=True)
        self.gg[2:3, 128:256] = jnp.sum(total_k, axis=0, keepdims=True)

    def project_back(self):
        for grad, first in ((self.dq2, 0), (self.dk2, 1024)):
            @pl.loop(0, 4)
            def _(j, grad=grad, first=first):
                cols = pl.ds(pl.multiple_of(first + j * 256, 256), 256)
                grad[rows_of(j, 256)] = dot_c(self.dp[:, cols], self.xn[...]).astype(BF)

    def d_normed(self, rows):
        return dot(self.dp[rows, 0:1024], self.wq2[...]) + dot(self.dp[rows, 1024:2048], self.wk2[...])

    def send_in(self):
        self.ls[...] = self.d_normed(self.theirs).astype(BF)
        self.share(16, self.ls, self.r0.at[pl.ds(256, 256)]).start()

    def finish_input(self):
        self.hid[0:256] = self.d_normed(self.mine)
        self.share(16, self.ls, self.r0.at[pl.ds(256, 256)]).wait()
        gain = self.gv[0:1, :]

        def body(i, total):
            r = rows_of(i, 64)
            at = pl.ds(pl.multiple_of(self.me.core * 256 + i * 64, 64), 64)
            over = pl.ds(pl.multiple_of(256 + i * 64, 64), 64)
            dz = self.hid[r] + self.r0[over].astype(F32)
            dv, term = norm_back(dz, self.xa[at].astype(F32), gain)
            self.igb[r] = (self.acc_d[at] + dv).astype(BF)
            return total + fold_rows(term)

        total = lax.fori_loop(0, 4, body, jnp.zeros((8, 1024), F32))
        self.gg[0:1, :] = jnp.sum(total, axis=0, keepdims=True)
        self.swap(17, self.igb, self.ig).start()

    def gains_flat(self):
        for i in range(8):
            cols = slice(i * 128, (i + 1) * 128)
            self.gs[i:i + 1, :] = self.gg[0:1, cols]
            self.gs[8 + i:9 + i, :] = self.gg[1:2, cols]
        self.gs[16:17, :] = self.gg[2:3, 0:128]
        self.gs[17:18, :] = self.gg[2:3, 128:256]
        self.gs[18:24, :] = jnp.zeros((6, 128), F32)


INPUTS = ("x_in", "ct_in", "meta_in", "wq_in", "wo_in", "wm_in", "gain_in", "consts")
OUTPUTS = ("lo", "ig", "oq", "oo", "om", "gs")
V, SEM = pltpu.VMEM, pltpu.SemaphoreType.DMA


def scratch():
    s = {"b" + k: V(SHAPES[k], BF) for k in KINDS}
    s.update(tq=V(SHAPES["q"], BF), tk=V(SHAPES["k"], BF))
    s.update(stage=V((4, 72, 256), F32))
    s.update(xa=V((512, 1024), BF), ct=V((512, 1024), BF), meta=V((2, 8, 256), jnp.int32), xn=V((512, 1024), BF))
    s.update(qp=V((512, 1024), BF), kp=V((512, 512), BF), qr=V((512, 1024), BF), kr=V((512, 512), BF), vl=V((512, 512), BF))
    s.update(cosine=V((512, 128), F32), sine=V((512, 128), F32), mask=V((512, 512), BF))
    s.update(p0=V((8, 256, 256), BF), p1=V((8, 256, 512), BF))
    s.update(hid=V((512, 1024), F32), acc_o=V((512, 1024), F32), acc_d=V((512, 1024), F32))
    s.update(r0=V((512, 1024), BF), r1=V((512, 1024), BF))
    s.update(ls=V((256, 1024), BF))
    s.update(dp=V((512, 2048), BF))
    s.update(ga=V((24, 128), F32), gv=V((8, 1024), F32), gg=V((8, 1024), F32), land_a=V((10, 24, 128), F32), land_b=V((10, 24, 128), F32))
    for k in KINDS:
        for p in range(3):
            s["land_%s%d" % (k, p)] = V((6,) + half_shape(k, ORDERS[k][:p], ORDERS[k][p]), BF)
        s["final_" + k] = V({"q": (2, 32, 256), "k": (2, 32, 256), "o": (2, 2, 16, 256)}.get(k, (2, 48, 256)), F32)
    for name, n in (("spread", 12), ("gather", 72), ("scatter", 108), ("collect", 20), ("small_a", 10), ("small_b", 10)):
        s[name + "_send"], s[name + "_recv"] = SEM((n,)), SEM((n,))
    s.update(spread_local=SEM((2,)), collect_local=SEM((5,)), xsend=SEM((18,)), xrecv=SEM((18,)), xlocal=SEM((18,)))
    return s


def kernel(*refs):
    shapes = scratch()
    S = dict(zip(INPUTS + OUTPUTS + tuple(shapes), refs))
    me = Place()
    greet(me)
    L = Layer(me, S)
    bufs = {k: S["b" + k] for k in KINDS}
    grads = dict(bufs, q=S["tq"], k=S["tk"])
    finals = {k: S["final_" + k] for k in KINDS}
    sp = Spread(me, S["wq_in"], S["wo_in"], S["wm_in"], bufs, S["stage"], S["spread_send"], S["spread_recv"], S["spread_local"])
    sp.start_attention()
    arrive = L.tokens_in()
    for c in arrive:
        c.start()
    sp.start_mlp()
    S["ga"][...] = S["gain_in"][...]
    ga = SmallSum(me, S["ga"], S["land_a"], S["small_a_send"], S["small_a_recv"])
    gb = SmallSum(me, S["gs"], S["land_b"], S["small_b_send"], S["small_b_recv"])
    G = {(k, p): Gather(me, k, p, bufs[k], S["gather_send"], S["gather_recv"], (KINDS.index(k) * 3 + p) * 4)
         for k in KINDS for p in range(3)}
    sp.wait_attention()

    def gather(rnd):
        for p in range(3):
            for act in ("start", "forward", "finish"):
                for k in rnd:
                    getattr(G[k, p], act)()

    gather("qko")
    sp.wait_mlp()
    gather("gud")
    for c in arrive:
        c.wait_recv()
    across = L.tokens_across()
    for c in across:
        c.start()
    for stage in range(4):
        ga.start(stage)
        ga.finish(stage)
    for c in across:
        c.wait()
    for c in arrive:
        c.wait_send()
    for k in KINDS:
        for p in range(3):
            G[k, p].drain()
    sp.drain()
    L.gains_rows()
    L.tables()
    L.norm_in()
    L.project()
    L.attend()
    L.out_project()
    L.norm_mid()
    L.acc_o[...] = jnp.zeros((512, 1024), F32)
    L.acc_d[...] = jnp.zeros((512, 1024), F32)
    pl.loop(0, 6)(L.feed_forward)
    L.send_mid()
    L.norm_mid_back()
    L.finish_output()
    L.out_back()
    L.attend_back()
    L.project_back()
    L.send_in()
    L.finish_input()
    L.gains_flat()
    C = Collect(me, S["oq"], S["oo"], S["om"], finals, S["collect_send"], S["collect_recv"], S["collect_local"])
    R = {(k, p): Scatter(me, k, p, grads[k], S["land_%s%d" % (k, p)], S["scatter_send"], S["scatter_recv"],
                         (KINDS.index(k) * 3 + p) * 6, finals[k] if p == 0 else None) for k in KINDS for p in range(3)}

    def scatter(rnd):
        for p in (2, 1, 0):
            for act in ("start", "forward", "finish", "drain"):
                for k in rnd:
                    getattr(R[k, p], act)()

    scatter("gud")
    for k in "gud":
        C.start(k)
    for stage in range(4):
        gb.start(stage)
        gb.finish(stage)
    scatter("qko")
    C.start("o")
    C.start("qk")
    for k in ("g", "u", "d", "o", "qk"):
        C.finish(k)
    for n, src, dst in ((15, L.lob, L.lo), (17, L.igb, L.ig)):
        c = L.swap(n, src, dst)
        c.wait_recv()
        c.wait_send()


def shards(layer_input, segments, positions, qkv_weight, out_weight, mlp_weight, gains, cotangent):
    place = lax.axis_index("seq") * 64 + lax.axis_index("dp")
    meta = jnp.concatenate([segments, positions, jnp.zeros((6, 256), jnp.int32)], axis=0)
    wm = jnp.transpose(mlp_weight, (1, 0, 2)).reshape(72, 1024).astype(F32)
    gain = lax.dynamic_update_slice(jnp.zeros((3072,), F32), gains.astype(F32), (place * 18,)).reshape(24, 128)
    freqs = THETA_BASE ** (-(jnp.arange(64, dtype=F32) * 2.0) / HEAD)
    sign = jnp.concatenate([-jnp.ones((64,), F32), jnp.ones((64,), F32)])
    consts = jnp.stack([jnp.concatenate([freqs, freqs]), sign] + [sign] * 6)
    vm = pl.BlockSpec(memory_space=pltpu.VMEM)
    shape = jax.ShapeDtypeStruct
    lo, ig, oq, oo, om, gs = pl.pallas_call(
        kernel,
        out_shape=(shape((256, 1024), BF), shape((256, 1024), BF), shape((32, 1024), F32), shape((16, 1024), F32),
                   shape((72, 1024), F32), shape((24, 128), F32)),
        in_specs=[vm] * len(INPUTS),
        out_specs=(vm,) * len(OUTPUTS),
        scratch_shapes=list(scratch().values()),
        compiler_params=pltpu.CompilerParams(collective_id=0, has_side_effects=True, vmem_limit_bytes=VMEM_BYTES),
    )(layer_input[0], cotangent[0], meta, qkv_weight.T, out_weight, wm, gain, consts)
    return (lo[None], ig[None], oq.T, oo, jnp.transpose(om.reshape(3, 24, 1024), (1, 0, 2)),
            lax.dynamic_slice(gs.reshape(3072), (place * 18,), (18,)))


def solution(mesh):
    rows, split = P("dp", "seq", None), ("seq", "dp")
    weights = (P(None, split), P(split, None), P(split, None, None), P(split))
    return jax.shard_map(shards, mesh=mesh, in_specs=(rows, P("dp", "seq"), P("dp", "seq")) + weights + (rows,),
                         out_specs=(rows, rows) + weights, check_vma=False)
```

```python
import math
import jax, jax.numpy as jnp
from jax import lax
from jax.experimental import pallas as pl
from jax.experimental.pallas import tpu as pltpu
from jax.sharding import PartitionSpec as P

MESH = pl.DeviceIdType.MESH
BF = jnp.bfloat16
F32 = jnp.float32
LQ = 256
HEAD = 128
EPSILON = 1e-06
THETA_BASE = 1000000.0
MASKED = -1e30
VMEM_BYTES = 63 << 20
SHAPES = {"q": (4, 2, 2, 2, 32, 1024), "k": (4, 2, 2, 2, 32, 1024), "o": (2, 2, 4, 2, 2, 16, 1024),
          **{k: (2, 4, 4, 48, 1024) for k in "gud"}}
ORDERS = {"q": "xyz", "k": "yzx", "o": "zxy", "g": "xyz", "u": "yzx", "d": "zxy"}
KINDS = "qkogud"
ATT, MLP = "qko", "gud"
PHASES = {k: [(0, None), (1, None)] + ([(2, 0), (2, 1)] if k in "gud" else [(2, None)]) for k in KINDS}


def pick(kind, x, y, z, h, chunk):
    every = slice(None)
    at = lambda v: every if v is None else v
    low = lambda v: every if v is None else v % 2
    high = lambda v: every if v is None else v // 2
    lanes = every if z is None else pl.ds(pl.multiple_of(z * LQ, LQ), LQ)
    if kind == "q":
        return (at(y), low(x), at(h), high(x), every, lanes)
    if kind == "k":
        return (at(y), high(x), at(h), low(x), every, lanes)
    if kind == "o":
        return (at(h), high(y), at(x), every, low(y), every, lanes)
    if h is not None:
        lanes = pl.ds(h * 512, 512) if z is None else pl.ds(pl.multiple_of(z * LQ + h * 128, 128), 128)
    return (at(chunk), at(x), at(y), every, lanes)


def half_shape(kind, full, axis, chunk):
    n = lambda a: 4 if a in full else None
    x, y, z = n("x"), n("y"), n("z")
    lanes = 1024 if z else 256
    if kind in "qk":
        s = ([4] if y else []) + ([2, 2] if x else []) + [32, lanes]
    elif kind == "o":
        s = ([2] if y else []) + ([4] if x else []) + [2] + ([2] if y else []) + [16, lanes]
    else:
        s = ([2] if chunk is None else []) + ([4] if x else []) + ([4] if y else []) + [48, lanes // 2]
    return tuple(s)


class Place:
    def __init__(self):
        s, d = lax.axis_index("seq"), lax.axis_index("dp")
        self.zlo, self.dp = s, d
        self.core = d % 2
        self.zhi = (d // 2) % 2
        self.x = (d // 4) % 4
        self.y = d // 16
        self.z = self.zhi * 2 + s

    def dev(self, x=None, y=None, z=None, core=None):
        x = self.x if x is None else x
        y = self.y if y is None else y
        z = self.z if z is None else z
        core = self.core if core is None else core
        return (z % 2, ((y * 4 + x) * 2 + z // 2) * 2 + core)

    def at(self, axis):
        return {"x": self.x, "y": self.y, "z": self.z}[axis]

    def ring(self, axis, step):
        return self.dev(**{axis: (self.at(axis) + step) % 4})


def flip(v):
    return v + 1 - 2 * (v % 2)


def block_rows(kind, phase, chunk):
    return 4 ** phase * (16 if kind in ATT else 24 if chunk is None else 12)


def ruler(ref, rows):
    for lanes in (1024, 768, 512, 256):
        n = rows * 1024 // lanes
        if rows * 1024 % lanes == 0 and n % 16 == 0 and n <= ref.shape[0]:
            return ref.at[pl.ds(0, n), pl.ds(0, lanes)]
    raise ValueError(rows)


def region(me, kind, full, axis, val, h=None, chunk=None):
    c = {a: (None if a in full else me.at(a)) for a in "xyz"}
    c[axis] = val
    return pick(kind, c["x"], c["y"], c["z"], h, chunk)


def remote(src, dst, send, recv, device):
    return pltpu.make_async_remote_copy(src_ref=src, dst_ref=dst, send_sem=send, recv_sem=recv, device_id=device, device_id_type=MESH)


class Phase:
    def __init__(self, me, kind, phase, chunk, buf, land, measure, send, recv, final=None):
        self.me, self.kind, self.chunk, self.buf, self.land, self.measure = me, kind, chunk, buf, land, measure
        self.send, self.recv, self.final = send, recv, final
        order = ORDERS[kind]
        self.axis, self.full = order[phase], order[:phase]
        self.rows = block_rows(kind, phase, chunk)
        self.small = phase == 0

    def idx(self, step, h=None):
        return region(self.me, self.kind, self.full, self.axis, (self.me.at(self.axis) + step + 4) % 4, h, self.chunk)

    def push(self, src, dst, n, hop):
        remote(src, dst, self.send, self.recv[n], self.me.ring(self.axis, hop % 4)).start()

    def take(self, n, regions):
        r = ruler(self.measure, self.rows * regions)
        remote(r, r, self.send, self.recv[n], self.me.ring(self.axis, 1)).wait_recv()


class Gather(Phase):
    def copy(self, step, h, n, hop):
        r = self.buf.at[self.idx(step, h)]
        self.push(r, r, n, hop)

    def start(self):
        self.copy(0, None, 0, 1)
        self.copy(0, None, 0, -1)
        if self.small:
            self.copy(0, None, 0, 2)

    def forward(self):
        self.take(0, 2)
        self.copy(-1, 0, 1, 1)
        self.copy(1, 1, 1, -1)

    def finish(self):
        self.take(0, 3) if self.small else self.take(1, 1)


class Scatter(Phase):
    def raw(self, to, step, h, n, hop):
        self.push(self.buf.at[self.idx(step, h)], self.land.at[to], n, hop)

    def start(self):
        if self.small:
            for step in (1, 3, 2):
                for h in range(2):
                    self.raw(2 * (step - 1) + h, step, h, 1, step)
            return
        self.raw(4, 2, 0, 0, 1)
        self.raw(5, 2, 1, 0, -1)
        self.raw(1, 1, 1, 1, 1)
        self.raw(3, -1, 0, 1, -1)

    def forward(self):
        self.take(0, 1)
        for at, step, h, to, hop in ((4, 1, 0, 0, 1), (5, -1, 1, 2, -1)):
            total = self.land[at].astype(F32) + self.buf[self.idx(step, h)].astype(F32)
            self.land[at] = total.astype(BF)
            self.push(self.land.at[at], self.land.at[to], 1, hop)

    def finish(self):
        self.take(1, 3 if self.small else 2)
        for h, slots in ((0, (0, 2, 4) if self.small else (0, 3)), (1, (1, 3, 5) if self.small else (2, 1))):
            total = self.buf[self.idx(0, h)].astype(F32)
            for a in slots:
                total = total + self.land[a].astype(F32)
            if self.final is None:
                self.buf[self.idx(0, h)] = total.astype(BF)
            elif self.kind in MLP:
                self.final[:, :, h * 128:(h + 1) * 128] = total
            else:
                self.final[h] = total


def greet(me):
    bar = pltpu.get_barrier_semaphore()
    x, y, z, c = me.x, me.y, me.z, me.core
    friends = [me.ring("x", s) for s in (1, 2, 3)] + [me.ring("y", s) for s in (1, 2, 3)] + [me.ring("z", s) for s in (1, 2, 3)]
    friends.append(me.dev(core=1 - c))
    for s in range(4):
        zz = (z + s) % 4
        friends.append(me.dev(x=(x + 2) % 4, z=zz, core=1 - c))
        friends.append(me.dev(x=flip(x), z=zz, core=1 - c))
        friends.append(me.dev(y=flip(y), z=zz, core=1 - c))
    friends.append(me.dev(z=flip(z), core=1 - c))
    for f in friends:
        pl.semaphore_signal(bar, inc=1, device_id=f, device_id_type=MESH)
    pl.semaphore_wait(bar, len(friends))


class Route:
    def __init__(self, own, src, dst, send, recv, local, device):
        self.own = own
        self.made_far = lambda: remote(src, dst, send, recv, device)
        self.made_near = lambda: pltpu.make_async_copy(src, dst, local)

    def start(self):
        if self.own is None:
            self.made_far().start()
        else:
            pl.when(self.own)(lambda: self.made_near().start())
            pl.when(jnp.logical_not(self.own))(lambda: self.made_far().start())

    def wait_recv(self):
        if self.own is None:
            self.made_far().wait_recv()
        else:
            pl.when(self.own)(lambda: self.made_near().wait())
            pl.when(jnp.logical_not(self.own))(lambda: self.made_far().wait_recv())

    def wait_send(self):
        if self.own is None:
            self.made_far().wait_send()
        else:
            pl.when(jnp.logical_not(self.own))(lambda: self.made_far().wait_send())


def mapping(me, kind):
    x, y, c = me.x, me.y, me.core
    if kind == "q":
        own = (c + x // 2 + 1) % 2
        return own, dict(x=(x + 2 * (1 - own)) % 4, y=y, core=(c + 1 - own) % 2)
    if kind == "k":
        own = (c + x + 1) % 2
        return own, dict(x=x + (1 - own) * (1 - 2 * (x % 2)), y=y, core=(c + 1 - own) % 2)
    own = (c + y + 1) % 2
    return own, dict(x=x, y=y + (1 - own) * (1 - 2 * (y % 2)), core=(c + 1 - own) % 2)


def lanes_of(z):
    return pl.ds(pl.multiple_of(z * LQ, LQ), LQ)


class Spread:
    def __init__(self, me, wq, wo, wm, bufs, stage, send, recv, local):
        self.me, self.wq, self.wo, self.wm, self.bufs, self.stage = me, wq, wo, wm, bufs, stage
        self.send, self.recv, self.local = send, recv, local

    def qk(self, kind, dz, zsrc, to=None):
        me = self.me
        own, col = mapping(me, kind)
        z = (me.z + dz) % 4
        place = dict(x=me.x, y=me.y) if to is None else col
        dst = self.bufs[kind].at[pick_piece(kind, place["x"], place["y"], z, zsrc)]
        n = zsrc // 2
        return Route((own == 1) & (zsrc == z), self.wq.at[:, lanes_of(z)], dst, self.send.at[dz],
                     self.recv.at[(0 if kind == "q" else 2) + n], self.local.at[0], me.dev(z=z, **col))

    def o(self, dz, zsrc, place):
        me = self.me
        own, col = mapping(me, "o")
        z = (me.z + dz) % 4
        y = me.y if place is None else col["y"]
        dst = self.bufs["o"].at[zsrc % 2, y // 2, me.x, zsrc // 2, y % 2, slice(None), lanes_of(z)]
        return Route((own == 1) & (zsrc == z), self.wo.at[:, lanes_of(z)], dst, self.send.at[4 + dz],
                     self.recv.at[4 + zsrc], self.local.at[1], me.dev(z=z, **col))

    def m(self, dz):
        me = self.me
        z = (me.z + dz) % 4
        return remote(self.wm.at[:, lanes_of(z)], self.stage.at[dz], self.send.at[8 + dz], self.recv.at[8 + dz], me.dev(z=z))

    def start_attention(self):
        me = self.me
        for kind, low in (("q", 0), ("k", 1)):
            @pl.when(me.zlo == low)
            def _(kind=kind):
                for dz in range(4):
                    self.qk(kind, dz, me.z, to=1).start()
        for dz in range(4):
            self.o(dz, me.z, 1).start()

    def start_mlp(self):
        for dz in range(1, 4):
            self.m(dz).start()

    def wait_attention(self):
        for n in range(2):
            self.qk("q", 0, 2 * n).wait_recv()
            self.qk("k", 0, 2 * n + 1).wait_recv()
        for zs in range(4):
            self.o(0, zs, None).wait_recv()

    def wait_mlp(self):
        me = self.me
        for dz in range(1, 4):
            self.m(dz).wait_recv()
        self.stage[0] = self.wm[:, lanes_of(me.z)]
        for t, kind in enumerate("gud"):
            rows = [self.stage[(me.z - zs + 4) % 4, t * 24:(t + 1) * 24, :] for zs in range(4)]
            block = jnp.concatenate(rows, axis=0).astype(BF)
            for j in range(2):
                self.bufs[kind][j, me.x, me.y, :, lanes_of(me.z)] = block[j * 48:(j + 1) * 48]

    def drain(self):
        me = self.me
        for kind, low in (("q", 0), ("k", 1)):
            @pl.when(me.zlo == low)
            def _(kind=kind):
                for dz in range(4):
                    self.qk(kind, dz, me.z, to=1).wait_send()
        for dz in range(4):
            self.o(dz, me.z, 1).wait_send()
        for dz in range(1, 4):
            self.m(dz).wait_send()


def pick_piece(kind, x, y, z, zsrc):
    every = slice(None)
    if kind == "q":
        return (y, x % 2, zsrc // 2, x // 2, every, lanes_of(z))
    return (y, x // 2, zsrc // 2, x % 2, every, lanes_of(z))


class Collect:
    def __init__(self, me, oq, oo, om, finals, send, recv, local):
        self.me, self.oq, self.oo, self.om, self.finals = me, oq, oo, om, finals
        self.send, self.recv, self.local = send, recv, local

    def qk(self, kind, dz):
        me = self.me
        own, col = mapping(me, kind)
        z = (me.z + dz) % 4
        keep = (own == 1) if dz == 0 else None
        return Route(keep, self.finals[kind].at[z // 2], self.oq.at[:, lanes_of(me.z)], self.send.at[dz],
                     self.recv.at[dz], self.local.at[0], me.dev(z=z, **col))

    def o(self, dz):
        me = self.me
        own, col = mapping(me, "o")
        z = (me.z + dz) % 4
        keep = (own == 1) if dz == 0 else None
        return Route(keep, self.finals["o"].at[z % 2, z // 2], self.oo.at[:, lanes_of(me.z)], self.send.at[4 + dz],
                     self.recv.at[4 + dz], self.local.at[1], me.dev(z=z, **col))

    def m(self, t, kind, dz):
        me = self.me
        z = (me.z + dz) % 4
        n = 8 + 4 * t + dz
        src = self.finals[kind].at[z // 2, pl.ds(pl.multiple_of((z % 2) * 24, 8), 24)]
        dst = self.om.at[pl.ds(t * 24, 24), lanes_of(me.z)]
        if dz == 0:
            return pltpu.make_async_copy(src, dst, self.local.at[2 + t])
        return remote(src, dst, self.send.at[n], self.recv.at[n], me.dev(z=z))

    def each_qk(self, act):
        me = self.me
        for dz in range(4):
            for kind, low in (("q", 0), ("k", 1)):
                @pl.when((me.z + dz) % 2 == low)
                def _(kind=kind, dz=dz):
                    act(self.qk(kind, dz))

    def start(self, kind):
        if kind == "qk":
            self.each_qk(lambda r: r.start())
        elif kind == "o":
            for dz in range(4):
                self.o(dz).start()
        else:
            for dz in range(4):
                self.m("gud".index(kind), kind, dz).start()

    def finish(self, kind):
        me = self.me
        if kind == "qk":
            for dz in range(4):
                for k, low in (("q", 0), ("k", 1)):
                    @pl.when(me.zlo == low)
                    def _(k=k, dz=dz):
                        self.qk(k, dz).wait_recv()
            self.each_qk(lambda r: r.wait_send())
        elif kind == "o":
            for dz in range(4):
                self.o(dz).wait_recv()
                self.o(dz).wait_send()
        else:
            for dz in range(4):
                c = self.m("gud".index(kind), kind, dz)
                if dz == 0:
                    c.wait()
                else:
                    c.wait_recv()
                    c.wait_send()


def dot(a, b):
    return jnp.dot(a, b, preferred_element_type=F32)


def dot_t(a, b):
    return lax.dot_general(a, b, (((1,), (1,)), ((), ())), preferred_element_type=F32)


def dot_c(a, b):
    return lax.dot_general(a, b, (((0,), (0,)), ((), ())), preferred_element_type=F32)


def mean_last(v):
    return jnp.mean(v, axis=-1, keepdims=True)


def norm_scale(v):
    return lax.rsqrt(mean_last(v * v) + EPSILON)


def norm_back(dz, v, gain):
    r = norm_scale(v)
    n = v * r
    w = dz * gain
    return r * (w - n * mean_last(w * n)), dz * n


def fold_rows(v):
    return jnp.sum(v.reshape(v.shape[0] // 8, 8, v.shape[1]), axis=0)


def rows_of(i, n):
    return pl.ds(pl.multiple_of(i * n, n), n)


class SmallSum:
    def __init__(self, me, buf, land, send, recv):
        self.me, self.buf, self.land, self.send, self.recv = me, buf, land, send, recv

    def copies(self, stage):
        if stage == 0:
            return [remote(self.buf, self.land.at[0], self.send.at[0], self.recv.at[0], self.me.dev(core=1 - self.me.core))]
        first = 1 + 3 * (stage - 1)
        return [remote(self.buf, self.land.at[first + s], self.send.at[stage], self.recv.at[stage],
                       self.me.ring("xyz"[stage - 1], s + 1)) for s in range(3)]

    def start(self, stage):
        for c in self.copies(stage):
            c.start()

    def finish(self, stage):
        if stage == 0:
            self.copies(0)[0].wait()
            self.buf[...] = self.buf[...] + self.land[0]
        else:
            first = 1 + 3 * (stage - 1)
            three = self.land.at[pl.ds(first, 3)]
            remote(three, three, self.send.at[stage], self.recv.at[stage], self.me.ring("xyz"[stage - 1], 1)).wait()
            self.buf[...] = self.buf[...] + (self.land[first] + self.land[first + 1] + self.land[first + 2])


class Layer:
    def __init__(self, me, S):
        self.me = me
        self.__dict__.update(S)
        c = me.core
        self.mine = rows_of(c, 256)
        self.theirs = rows_of(1 - c, 256)
        self.peer = me.dev(core=1 - c)
        self.wq2 = self.bq.reshape(1024, 1024)
        self.wk2 = self.bk.reshape(1024, 1024)
        self.wo2 = self.bo.reshape(1024, 1024)
        self.mlp = [[S["b" + k].at[j].reshape(768, 1024) for k in "gud"] for j in range(2)]
        self.dq2 = self.tq.reshape(1024, 1024)
        self.dk2 = self.tk.reshape(1024, 1024)
        self.cx, self.mi = self.dq2.at[pl.ds(0, 512)], self.dq2.at[pl.ds(512, 512)]
        self.es = self.dp.at[:, pl.ds(0, 1024)]
        self.lob, self.igb = self.ct.at[pl.ds(0, 256)], self.ct.at[pl.ds(256, 256)]
        self.da, self.dc = self.dk2.at[pl.ds(0, 512)], self.dk2.at[pl.ds(512, 512)]

    def swap(self, n, src, dst):
        me = self.me
        return Route(me.core == me.zlo, src, dst, self.xsend.at[n], self.xrecv.at[n], self.xlocal.at[n],
                     me.dev(z=me.zhi * 2 + me.core, core=me.zlo))

    def share(self, n, src, dst):
        return remote(src, dst, self.xsend.at[n], self.xrecv.at[n], self.peer)

    def tokens_in(self):
        there = self.me.zlo
        return [self.swap(0, self.x_in, self.xa.at[rows_of(there, 256)]),
                self.swap(1, self.seg_in, self.seg.at[there]),
                self.swap(2, self.pos_in, self.pos.at[there]),
                self.swap(3, self.ct_in, self.ct.at[rows_of(there, 256)])]

    def send_piece(self, n, i):
        src, dst = (self.x_in, self.xa) if n == 0 else (self.ct_in, self.ct)
        self.swap(n, src.at[pl.ds(i * 64, 64)], dst.at[pl.ds(pl.multiple_of(self.me.zlo * 256 + i * 64, 64), 64)]).start()

    def tokens_across(self):
        m = self.mine
        c = self.me.core
        return [self.share(4, self.xa.at[m], self.xa.at[m]),
                self.share(5, self.seg.at[c], self.seg.at[c]),
                self.share(6, self.pos.at[c], self.pos.at[c]),
                self.share(7, self.ct.at[m], self.ct.at[m])]

    def gains_rows(self):
        for i in range(8):
            cols = slice(i * 128, (i + 1) * 128)
            self.gv[0:1, cols] = self.ga[i:i + 1, :]
            self.gv[1:2, cols] = self.ga[8 + i:9 + i, :]
        self.gv[2:3, 0:128] = self.ga[16:17, :]
        self.gv[2:3, 128:256] = self.ga[17:18, :]

    def tables(self):
        lane = lax.broadcasted_iota(jnp.int32, (1, 128), 1)
        freqs = jnp.exp((lane % 64).astype(F32) * (-2.0 * math.log(THETA_BASE) / HEAD))
        sign = jnp.where(lane < 64, -1.0, 1.0)
        for h in range(2):
            angle = jnp.broadcast_to(self.pos[h].astype(F32), (128, 256)).T * freqs
            self.cosine[h * 256:(h + 1) * 256] = jnp.cos(angle)
            self.sine[h * 256:(h + 1) * 256] = jnp.sin(angle) * sign
        for q in range(2):
            seg_q = jnp.broadcast_to(self.seg[q].astype(F32), (128, 256)).T[:, 0:1]
            for k in range(2):
                seg_k = self.seg[k].astype(F32)
                row = lax.broadcasted_iota(jnp.int32, (256, 256), 0) + q * 256
                col = lax.broadcasted_iota(jnp.int32, (256, 256), 1) + k * 256
                allowed = (seg_q == seg_k) & (col <= row)
                self.mask[q * 256:(q + 1) * 256, k * 256:(k + 1) * 256] = jnp.where(allowed, 0.0, MASKED).astype(BF)

    def norm_in(self):
        gain = self.gv[0:1, :]

        @pl.loop(0, 8)
        def _(i):
            r = rows_of(i, 64)
            v = self.xa[r].astype(F32)
            self.xn[r] = (v * norm_scale(v) * gain).astype(BF)

    def rope(self, n):
        return n * self.cosine[...] + pltpu.roll(n, 64, 1) * self.sine[...]

    def unrope(self, d, rows):
        return d * self.cosine[rows] - pltpu.roll(d, 64, 1) * self.sine[rows]

    def project(self):
        gq, gk = self.gv[2:3, 0:128], self.gv[2:3, 128:256]

        @pl.loop(0, 4)
        def _(i):
            pre = dot_t(self.xn[...], self.wq2[rows_of(i, 256)])
            for g in range(2):
                v = pre[:, g * 128:(g + 1) * 128]
                cols = pl.ds(pl.multiple_of(i * 256 + g * 128, 128), 128)
                self.qp[:, cols] = v.astype(BF)
                self.qr[:, cols] = self.rope(v * norm_scale(v) * gq).astype(BF)

        @pl.loop(0, 2)
        def _(i):
            pre = dot_t(self.xn[...], self.wk2[rows_of(i, 256)])
            for g in range(2):
                v = pre[:, g * 128:(g + 1) * 128]
                cols = pl.ds(pl.multiple_of(i * 256 + g * 128, 128), 128)
                self.kp[:, cols] = v.astype(BF)
                self.kr[:, cols] = self.rope(v * norm_scale(v) * gk).astype(BF)
            self.vl[:, rows_of(i, 256)] = dot_t(self.xn[...], self.wk2[rows_of(i + 2, 256)]).astype(BF)

    def attend(self):
        factor = HEAD ** -0.5 * 1.4426950408889634

        @pl.loop(0, 4)
        def _(k):
            kcols = rows_of(k, 128)
            for b in range(2):
                n = 256 * (b + 1)
                rows = slice(b * 256, (b + 1) * 256)
                keys, values = self.kr[0:n, kcols], self.vl[0:n, kcols]
                for g in range(2):
                    qcols = pl.ds(pl.multiple_of(k * 256 + g * 128, 128), 128)
                    s = dot_t(self.qr[rows, qcols], keys)
                    p = jnp.exp2(s * factor + self.mask[rows, 0:n].astype(F32))
                    p = (p * (1.0 / jnp.sum(p, axis=-1, keepdims=True))).astype(BF)
                    (self.p0 if b == 0 else self.p1)[2 * k + g] = p
                    self.cx[rows, qcols] = dot(p, values).astype(BF)

    def exchange(self, n, chunk, land):
        cols = slice(chunk * 256, (chunk + 1) * 256)
        return self.share(n + chunk, self.es.at[:, cols], land.at[:, cols])

    def out_project(self):
        for j in range(4):
            cols = slice(j * 256, (j + 1) * 256)
            part = dot(self.cx[...], self.wo2[:, cols])
            self.es[:, cols] = part.astype(BF)
            self.exchange(8, j, self.r0).start()
            self.hid[:, cols] = part + self.xa[:, cols].astype(F32)

    def norm_mid(self):
        for j in range(4):
            self.exchange(8, j, self.r0).wait()
        gain = self.gv[1:2, :]

        @pl.loop(0, 8)
        def _(i):
            r = rows_of(i, 64)
            v = self.hid[r] + self.r0[r].astype(F32)
            self.hid[r] = v
            self.mi[r] = (v * norm_scale(v) * gain).astype(BF)

    def feed_forward(self, j, c):
        wg2, wu2, wd2 = self.mlp[j]
        r = rows_of(c, 256)
        gate = dot_t(self.mi[...], wg2[r])
        up = dot_t(self.mi[...], wu2[r])
        back = dot_t(self.ct[...], wd2[r])
        sig = jax.nn.sigmoid(gate)
        silu = gate * sig
        act = (silu * up).astype(BF)
        d_gate = (back * up * sig * (1.0 + gate * (1.0 - sig))).astype(BF)
        d_up = (back * silu).astype(BF)
        self.acc_o[...] += dot(act, wd2[r])
        self.acc_d[...] += dot(d_gate, wg2[r]) + dot(d_up, wu2[r])
        wd2[r] = dot_c(act, self.ct[...]).astype(BF)
        wg2[r] = dot_c(d_gate, self.mi[...]).astype(BF)
        wu2[r] = dot_c(d_up, self.mi[...]).astype(BF)

    def send_mid(self):
        self.es[...] = self.acc_d[...].astype(BF)
        for j in range(4):
            self.exchange(12, j, self.r1).start()

    def norm_mid_back(self):
        for j in range(4):
            self.exchange(12, j, self.r1).wait()
        gain = self.gv[1:2, :]

        def body(i, total):
            r = rows_of(i, 64)
            dz = self.acc_d[r] + self.r1[r].astype(F32)
            dv, term = norm_back(dz, self.hid[r], gain)
            d = self.ct[r].astype(F32) + dv
            self.acc_d[r] = d
            self.da[r] = d.astype(BF)
            return total + fold_rows(term) * (i // 4 == self.me.core).astype(F32)

        total = lax.fori_loop(0, 8, body, jnp.zeros((8, 1024), F32))
        self.gg[1:2, :] = jnp.sum(total, axis=0, keepdims=True)

    def finish_output(self):
        self.ls[...] = self.acc_o[self.theirs].astype(BF)
        self.share(16, self.ls, self.r0.at[pl.ds(0, 256)]).start()
        self.share(16, self.ls, self.r0.at[pl.ds(0, 256)]).wait()
        self.lob[...] = (self.acc_o[self.mine] + self.hid[self.mine] + self.r0[0:256].astype(F32)).astype(BF)

    def out_back(self):
        for j in range(4):
            r = slice(j * 256, (j + 1) * 256)
            self.dc[:, r] = dot_t(self.da[...], self.wo2[r]).astype(BF)
        for j in range(4):
            r = slice(j * 256, (j + 1) * 256)
            self.wo2[r] = dot_c(self.cx[:, r], self.da[...]).astype(BF)

    def attend_back(self, between):
        scale = HEAD ** -0.5
        gq, gk = self.gv[2:3, 0:128], self.gv[2:3, 128:256]

        def body(k, totals):
            total_q, total_k = totals
            kcols = rows_of(k, 128)
            dk, dv = [0.0, 0.0], [0.0, 0.0]
            for b in range(2):
                n = 256 * (b + 1)
                rows = slice(b * 256, (b + 1) * 256)
                keys, values = self.kr[0:n, kcols], self.vl[0:n, kcols]
                for g in range(2):
                    qcols = pl.ds(pl.multiple_of(k * 256 + g * 128, 128), 128)
                    low = (self.p0 if b == 0 else self.p1)[2 * k + g]
                    dc = self.dc[rows, qcols]
                    p = low.astype(F32)
                    t = p * dot_t(dc, values)
                    ds = (t - p * jnp.sum(t, axis=-1, keepdims=True)).astype(BF)
                    dz = self.unrope(dot(ds, keys) * scale, rows)
                    dq, term = norm_back(dz, self.qp[rows, qcols].astype(F32), gq)
                    self.dp[rows, qcols] = dq.astype(BF)
                    total_q = total_q + fold_rows(term)
                    pk, pv = dot_c(ds, self.qr[rows, qcols]), dot_c(low, dc)
                    for j in range(b + 1):
                        part = slice(j * 256, (j + 1) * 256)
                        dk[j] = dk[j] + pk[part]
                        dv[j] = dv[j] + pv[part]
            for j in range(2):
                rows = slice(j * 256, (j + 1) * 256)
                dz = self.unrope(dk[j] * scale, rows)
                dkey, term = norm_back(dz, self.kp[rows, kcols].astype(F32), gk)
                self.dp[rows, pl.ds(pl.multiple_of(1024 + k * 128, 128), 128)] = dkey.astype(BF)
                self.dp[rows, pl.ds(pl.multiple_of(1536 + k * 128, 128), 128)] = dv[j].astype(BF)
                total_k = total_k + fold_rows(term)
            between(k)
            return total_q, total_k

        zero = jnp.zeros((8, 128), F32)
        total_q, total_k = lax.fori_loop(0, 4, body, (zero, zero))
        self.gg[2:3, 0:128] = jnp.sum(total_q, axis=0, keepdims=True)
        self.gg[2:3, 128:256] = jnp.sum(total_k, axis=0, keepdims=True)

    def project_back(self, kind):
        grad, first = (self.dq2, 0) if kind == "q" else (self.dk2, 1024)

        @pl.loop(0, 4)
        def _(j):
            cols = pl.ds(pl.multiple_of(first + j * 256, 256), 256)
            grad[rows_of(j, 256)] = dot_c(self.dp[:, cols], self.xn[...]).astype(BF)

    def d_normed(self, rows):
        return dot(self.dp[rows, 0:1024], self.wq2[...]) + dot(self.dp[rows, 1024:2048], self.wk2[...])

    def send_in(self):
        self.ls[...] = self.d_normed(self.theirs).astype(BF)
        self.share(18, self.ls, self.r0.at[pl.ds(256, 256)]).start()

    def finish_input(self):
        self.hid[0:256] = self.d_normed(self.mine)
        self.share(18, self.ls, self.r0.at[pl.ds(256, 256)]).wait()
        gain = self.gv[0:1, :]

        def body(i, total):
            r = rows_of(i, 64)
            at = pl.ds(pl.multiple_of(self.me.core * 256 + i * 64, 64), 64)
            over = pl.ds(pl.multiple_of(256 + i * 64, 64), 64)
            dz = self.hid[r] + self.r0[over].astype(F32)
            dv, term = norm_back(dz, self.xa[at].astype(F32), gain)
            self.igb[r] = (self.acc_d[at] + dv).astype(BF)
            return total + fold_rows(term)

        total = lax.fori_loop(0, 4, body, jnp.zeros((8, 1024), F32))
        self.gg[0:1, :] = jnp.sum(total, axis=0, keepdims=True)

    def gains_flat(self):
        for i in range(8):
            cols = slice(i * 128, (i + 1) * 128)
            self.gs[i:i + 1, :] = self.gg[0:1, cols]
            self.gs[8 + i:9 + i, :] = self.gg[1:2, cols]
        self.gs[16:17, :] = self.gg[2:3, 0:128]
        self.gs[17:18, :] = self.gg[2:3, 128:256]
        self.gs[18:24, :] = jnp.zeros((6, 128), F32)


INPUTS = ("x_in", "ct_in", "seg_in", "pos_in", "wq_in", "wo_in", "wm_in", "gain_in")
OUTPUTS = ("lo", "ig", "oq", "oo", "om", "gs")
V, SEM = pltpu.VMEM, pltpu.SemaphoreType.DMA


def scratch():
    s = {"b" + k: V(SHAPES[k], BF) for k in KINDS}
    s.update(tq=V(SHAPES["q"], BF), tk=V(SHAPES["k"], BF))
    s.update(stage=V((4, 72, 256), F32), wqt=V((32, 1024), BF), wov=V((16, 1024), BF), wmv=V((3, 24, 1024), BF), wmf=V((72, 1024), F32))
    s.update(xa=V((512, 1024), BF), ct=V((512, 1024), BF), seg=V((2, 1, 256), jnp.int32), pos=V((2, 1, 256), jnp.int32), xn=V((512, 1024), BF))
    s.update(qp=V((512, 1024), BF), kp=V((512, 512), BF), qr=V((512, 1024), BF), kr=V((512, 512), BF), vl=V((512, 512), BF))
    s.update(cosine=V((512, 128), F32), sine=V((512, 128), F32), mask=V((512, 512), BF))
    s.update(p0=V((8, 256, 256), BF), p1=V((8, 256, 512), BF))
    s.update(hid=V((512, 1024), F32), acc_o=V((512, 1024), F32), acc_d=V((512, 1024), F32))
    s.update(r0=V((512, 1024), BF), r1=V((512, 1024), BF))
    s.update(ls=V((256, 1024), BF))
    s.update(dp=V((512, 2048), BF))
    s.update(ga=V((24, 128), F32), gv=V((8, 1024), F32), gg=V((8, 1024), F32), land_a=V((10, 24, 128), F32), land_b=V((10, 24, 128), F32))
    for k in KINDS:
        order = ORDERS[k]
        for n, (p, chunk) in enumerate(PHASES[k]):
            s["land_%s%d" % (k, n)] = V((6,) + half_shape(k, order[:p], order[p], chunk), BF)
    for k in "qkogud":
        s["final_" + k] = V({"q": (2, 32, 256), "k": (2, 32, 256), "o": (2, 2, 16, 256)}.get(k, (2, 48, 256)), F32)
    phases = 2 * sum(len(p) for p in PHASES.values())
    for name, n in (("spread", 12), ("collect", 20), ("small_a", 4), ("small_b", 4)):
        s[name + "_send"], s[name + "_recv"] = SEM((n,)), SEM((n,))
    s.update(gather_recv=SEM((phases,)), scatter_recv=SEM((phases,)))
    s.update(spread_local=SEM((2,)), collect_local=SEM((5,)), xsend=SEM((20,)), xrecv=SEM((20,)), xlocal=SEM((20,)), drained=SEM((4 * len(KINDS),)), fetch=SEM((3,)))
    return s


def kernel(*refs):
    shapes = scratch()
    S = dict(zip(INPUTS + OUTPUTS + tuple(shapes), refs))
    me = Place()
    fetch = [pltpu.make_async_copy(S[a], S[b], S["fetch"].at[n]) for n, (a, b) in
             enumerate((("wq_in", "wqt"), ("wo_in", "wov"), ("wm_in", "wmv")))]
    for c in fetch:
        c.start()
    greet(me)
    L = Layer(me, S)
    bufs = {k: S["b" + k] for k in KINDS}
    grads = dict(bufs, q=S["tq"], k=S["tk"])
    finals = {k: S["final_" + k] for k in "qkogud"}
    sp = Spread(me, S["wqt"], S["wov"], S["wmf"], bufs, S["stage"], S["spread_send"], S["spread_recv"], S["spread_local"])
    ga = SmallSum(me, S["ga"], S["land_a"], S["small_a_send"], S["small_a_recv"])
    gb = SmallSum(me, S["gs"], S["land_b"], S["small_b_send"], S["small_b_recv"])
    C = Collect(me, S["oq"], S["oo"], S["om"], finals, S["collect_send"], S["collect_recv"], S["collect_local"])
    gathers, scatters, sent, n = {}, {}, S["drained"], 0
    measure = S["bg"].reshape(1536, 1024)
    for i, k in enumerate(KINDS):
        for j, (p, chunk) in enumerate(PHASES[k]):
            two = lambda name: (S[name].at[2 * n], S[name].at[2 * n + 1])
            gathers[k, p, chunk] = Gather(me, k, p, chunk, bufs[k], None, measure, sent.at[2 * i + (chunk == 1)], two("gather_recv"))
            scatters[k, p, chunk] = Scatter(me, k, p, chunk, grads[k], S["land_%s%d" % (k, j)], measure,
                                            sent.at[12 + 2 * i + (chunk is not None)], two("scatter_recv"), finals[k] if p == 0 else None)
            n += 1

    def drain(sem, rows):
        r = ruler(measure, rows)
        remote(r, r, sem, S["gather_recv"].at[0], me.ring("x", 1)).wait_send()

    def run(table, kinds, p, chunk, acts):
        for act in acts:
            for k in kinds:
                getattr(table[k, p, chunk], act)()

    def G(kinds, p, *acts, chunk=None):
        run(gathers, kinds, p, chunk, acts)

    def R(kinds, p, *acts, chunk=None):
        run(scatters, kinds, p, chunk, acts)

    arrive = L.tokens_in()
    across = L.tokens_across()
    fetch[0].wait()
    fetch[1].wait()
    sp.start_attention()
    arrive[1].start()
    arrive[2].start()
    L.send_piece(0, 0)
    L.send_piece(0, 1)
    first = 18 * (me.zlo * 64 + me.dp)
    wide = jnp.concatenate([S["gain_in"][...].astype(F32), jnp.zeros((1, 238), F32)], axis=1)
    wide = pltpu.roll(jnp.broadcast_to(wide, (8, 256)), first % 128, 1)[0:1]
    S["ga"][...] = jnp.zeros((24, 128), F32)
    S["ga"][pl.ds(first // 128, 1), :] = wide[:, 0:128]
    S["ga"][pl.ds(first // 128 + 1, 1), :] = wide[:, 128:256]
    ga.start(0)
    fetch[2].wait()
    for t in range(3):
        S["wmf"][t * 24:(t + 1) * 24, :] = S["wmv"][t].astype(F32)
    sp.start_mlp()
    sp.wait_attention()
    G(ATT, 0, "start")
    ga.finish(0)
    ga.start(1)
    L.send_piece(0, 2)
    L.send_piece(0, 3)
    sp.wait_mlp()
    G(MLP, 0, "start")
    G(ATT, 0, "finish")
    G(ATT, 1, "start")
    L.send_piece(3, 0)
    ga.finish(1)
    ga.start(2)
    L.acc_o[...] = jnp.zeros((512, 1024), F32)
    L.acc_d[...] = jnp.zeros((512, 1024), F32)
    G(MLP, 0, "finish")
    G(ATT, 1, "forward")
    G(MLP, 1, "start")
    ga.finish(2)
    ga.start(3)
    for c in arrive[:3]:
        c.wait_recv()
    for c in across[:3]:
        c.start()
    G(ATT, 1, "finish")
    G(ATT, 2, "start")
    G(MLP, 1, "forward")
    ga.finish(3)
    L.gains_rows()
    for c in across[:3]:
        c.wait()
    L.tables()
    L.norm_in()
    G(ATT, 2, "forward")
    for i in range(1, 4):
        L.send_piece(3, i)
    G(MLP, 1, "finish")
    G(MLP, 2, "start", chunk=0)
    G(ATT, 2, "finish")
    L.project()
    arrive[3].wait_recv()
    across[3].start()
    G(MLP, 2, "forward", chunk=0)
    G(MLP, 2, "start", chunk=1)
    L.attend()
    L.out_project()
    across[3].wait()
    for c in arrive:
        c.wait_send()
    sp.drain()
    L.norm_mid()
    G(MLP, 2, "finish", chunk=0)
    for i, k in enumerate(KINDS):
        drain(sent.at[2 * i], 63 * 16 if k in ATT else 3 * 24 + 12 * 24 + 48 * 12)

    @pl.loop(0, 3)
    def _(c):
        L.feed_forward(0, c)

        @pl.when(c == 0)
        def _():
            G(MLP, 2, "forward", chunk=1)

    R(MLP, 2, "start", chunk=0)
    G(MLP, 2, "finish", chunk=1)
    for i in range(3, 6):
        drain(sent.at[2 * i + 1], 48 * 12)

    @pl.loop(0, 3)
    def _(c):
        L.feed_forward(1, c)

    R(MLP, 2, "forward", chunk=0)
    R(MLP, 2, "start", chunk=1)
    L.send_mid()
    L.norm_mid_back()
    R(MLP, 2, "finish", chunk=0)
    L.finish_output()
    L.out_back()
    R(MLP, 2, "forward", chunk=1)
    L.swap(17, L.lob, L.lo).start()
    R("o", 2, "start")

    def between(k):
        @pl.when(k == 2)
        def _():
            R(MLP, 2, "finish", chunk=1)
            R(MLP, 1, "start")

    L.attend_back(between)
    L.project_back("q")
    R("q", 2, "start")
    R("o", 2, "forward")
    L.project_back("k")
    R("k", 2, "start")
    L.send_in()
    R(MLP, 1, "forward")
    L.finish_input()
    R("q", 2, "forward")
    R("k", 2, "forward")
    L.gains_flat()
    gb.start(0)
    R(MLP, 1, "finish")
    R(MLP, 0, "start")
    R("o", 2, "finish")
    R("o", 1, "start")
    gb.finish(0)
    gb.start(1)
    R("q", 2, "finish")
    R("q", 1, "start")
    R("k", 2, "finish")
    R("k", 1, "start")
    R("o", 1, "forward")
    gb.finish(1)
    gb.start(2)
    R(MLP, 0, "finish")
    for k in MLP:
        C.start(k)
    R("q", 1, "forward")
    R("k", 1, "forward")
    L.swap(19, L.igb, L.ig).start()
    R("o", 1, "finish")
    R("o", 0, "start")
    R("q", 1, "finish")
    R("q", 0, "start")
    R("k", 1, "finish")
    R("k", 0, "start")
    gb.finish(2)
    gb.start(3)
    R("o", 0, "finish")
    C.start("o")
    R("qk", 0, "finish")
    C.start("qk")
    gb.finish(3)
    for k in ("g", "u", "d", "o", "qk"):
        C.finish(k)
    for i, k in enumerate(KINDS):
        if k in ATT:
            drain(sent.at[12 + 2 * i], 63 * 16)
        else:
            drain(sent.at[12 + 2 * i], 15 * 24)
            drain(sent.at[13 + 2 * i], 96 * 12)
    for n, src, dst in ((17, L.lob, L.lo), (19, L.igb, L.ig)):
        c = L.swap(n, src, dst)
        c.wait_recv()
        c.wait_send()


def finish_kernel(*refs):
    given, gs, outs, gain_out, held, sem = refs[:5], refs[5], refs[6:11], refs[11], refs[12:17], refs[17]
    loads = [pltpu.make_async_copy(a, b, sem.at[n]) for n, (a, b) in enumerate(zip(given, held))]
    stores = [pltpu.make_async_copy(a, b, sem.at[5 + n]) for n, (a, b) in enumerate(zip(held, outs))]
    for m in loads:
        m.start()
    first = 18 * (lax.axis_index("seq") * 64 + lax.axis_index("dp"))
    wide = jnp.concatenate([gs[pl.ds(first // 128, 1), :], gs[pl.ds(first // 128 + 1, 1), :]], axis=1)
    wide = pltpu.roll(jnp.broadcast_to(wide, (8, 256)), 256 - first % 128, 1)
    gain_out[...] = wide[0:1, 0:18]
    for load, store in zip(loads, stores):
        load.wait()
        store.start()
    for m in stores:
        m.wait()


def shards(layer_input, segments, positions, qkv_weight, out_weight, mlp_weight, gains, cotangent):
    vm, hbm = pl.BlockSpec(memory_space=pltpu.VMEM), pl.BlockSpec(memory_space=pl.ANY)
    shape = jax.ShapeDtypeStruct
    lo, ig, oq, oo, om, gs = pl.pallas_call(
        kernel,
        out_shape=(shape((256, 1024), BF), shape((256, 1024), BF), shape((32, 1024), F32), shape((16, 1024), F32),
                   shape((72, 1024), F32), shape((24, 128), F32)),
        in_specs=[hbm] * 7 + [vm],
        out_specs=(hbm,) * 5 + (vm,),
        scratch_shapes=list(scratch().values()),
        compiler_params=pltpu.CompilerParams(collective_id=0, has_side_effects=True, vmem_limit_bytes=VMEM_BYTES),
    )(layer_input[0], cotangent[0], segments, positions, qkv_weight.T, out_weight, jnp.transpose(mlp_weight, (1, 0, 2)), gains.reshape(1, 18))
    lo, ig, oq, oo, om, gs = pl.pallas_call(
        finish_kernel,
        out_shape=(shape((256, 1024), BF), shape((256, 1024), BF), shape((32, 1024), F32), shape((16, 1024), F32),
                   shape((72, 1024), F32), shape((1, 18), F32)),
        in_specs=[hbm] * 5 + [vm],
        out_specs=(hbm,) * 5 + (vm,),
        scratch_shapes=[V((256, 1024), BF), V((256, 1024), BF), V((32, 1024), F32), V((16, 1024), F32), V((72, 1024), F32), SEM((10,))],
    )(lo, ig, oq, oo, om, gs)
    return lo[None], ig[None], oq.T, oo, jnp.transpose(om.reshape(3, 24, 1024), (1, 0, 2)), gs.reshape(18)


def solution(mesh):
    rows, split = P("dp", "seq", None), ("seq", "dp")
    weights = (P(None, split), P(split, None), P(split, None, None), P(split))
    return jax.shard_map(shards, mesh=mesh, in_specs=(rows, P("dp", "seq"), P("dp", "seq")) + weights + (rows,),
                         out_specs=(rows, rows) + weights, check_vma=False)
```

```python
import math
import jax, jax.numpy as jnp
from jax import lax
from jax.experimental import pallas as pl
from jax.experimental.pallas import tpu as pltpu
from jax.sharding import PartitionSpec as P

MESH = pl.DeviceIdType.MESH
BF = jnp.bfloat16
F32 = jnp.float32
LQ = 256
HEAD = 128
EPSILON = 1e-06
THETA_BASE = 1000000.0
MASKED = -1e30
VMEM_BYTES = 63 << 20
SHAPES = {"q": (4, 2, 2, 2, 32, 1024), "k": (4, 2, 2, 2, 32, 1024), "o": (2, 2, 4, 2, 2, 16, 1024),
          **{k: (2, 4, 4, 48, 1024) for k in "gud"}}
ORDERS = {"q": "xyz", "k": "yzx", "o": "zxy", "g": "xyz", "u": "yzx", "d": "zxy"}
KINDS = "qkogud"
ATT, MLP = "qko", "gud"
PHASES = {k: [(0, None), (1, None)] + ([(2, 0), (2, 1)] if k in "gud" else [(2, None)]) for k in KINDS}


def pick(kind, x, y, z, h, chunk):
    every = slice(None)
    at = lambda v: every if v is None else v
    low = lambda v: every if v is None else v % 2
    high = lambda v: every if v is None else v // 2
    lanes = every if z is None else pl.ds(pl.multiple_of(z * LQ, LQ), LQ)
    if kind == "q":
        return (at(y), low(x), at(h), high(x), every, lanes)
    if kind == "k":
        return (at(y), high(x), at(h), low(x), every, lanes)
    if kind == "o":
        return (at(h), high(y), at(x), every, low(y), every, lanes)
    if h is not None:
        lanes = pl.ds(h * 512, 512) if z is None else pl.ds(pl.multiple_of(z * LQ + h * 128, 128), 128)
    return (at(chunk), at(x), at(y), every, lanes)


def half_shape(kind, full, axis, chunk):
    n = lambda a: 4 if a in full else None
    x, y, z = n("x"), n("y"), n("z")
    lanes = 1024 if z else 256
    if kind in "qk":
        s = ([4] if y else []) + ([2, 2] if x else []) + [32, lanes]
    elif kind == "o":
        s = ([2] if y else []) + ([4] if x else []) + [2] + ([2] if y else []) + [16, lanes]
    else:
        s = ([2] if chunk is None else []) + ([4] if x else []) + ([4] if y else []) + [48, lanes // 2]
    return tuple(s)


class Place:
    def __init__(self):
        s, d = lax.axis_index("seq"), lax.axis_index("dp")
        self.zlo, self.dp = s, d
        self.core = d % 2
        self.zhi = (d // 2) % 2
        self.x = (d // 4) % 4
        self.y = d // 16
        self.z = self.zhi * 2 + s

    def dev(self, x=None, y=None, z=None, core=None):
        x = self.x if x is None else x
        y = self.y if y is None else y
        z = self.z if z is None else z
        core = self.core if core is None else core
        return (z % 2, ((y * 4 + x) * 2 + z // 2) * 2 + core)

    def at(self, axis):
        return {"x": self.x, "y": self.y, "z": self.z}[axis]

    def ring(self, axis, step):
        return self.dev(**{axis: (self.at(axis) + step) % 4})


def flip(v):
    return v + 1 - 2 * (v % 2)


def block_rows(kind, phase, chunk):
    return 4 ** phase * (16 if kind in ATT else 24 if chunk is None else 12)


def ruler(ref, rows):
    for lanes in (1024, 768, 512, 256):
        n = rows * 1024 // lanes
        if rows * 1024 % lanes == 0 and n % 16 == 0 and n <= ref.shape[0]:
            return ref.at[pl.ds(0, n), pl.ds(0, lanes)]
    raise ValueError(rows)


def region(me, kind, full, axis, val, h=None, chunk=None):
    c = {a: (None if a in full else me.at(a)) for a in "xyz"}
    c[axis] = val
    return pick(kind, c["x"], c["y"], c["z"], h, chunk)


def remote(src, dst, send, recv, device):
    return pltpu.make_async_remote_copy(src_ref=src, dst_ref=dst, send_sem=send, recv_sem=recv, device_id=device, device_id_type=MESH)


class Phase:
    def __init__(self, me, kind, phase, chunk, buf, land, measure, send, recv, final=None):
        self.me, self.kind, self.chunk, self.buf, self.land, self.measure = me, kind, chunk, buf, land, measure
        self.send, self.recv, self.final = send, recv, final
        order = ORDERS[kind]
        self.axis, self.full = order[phase], order[:phase]
        self.rows = block_rows(kind, phase, chunk)
        self.small = phase == 0

    def idx(self, step, h=None):
        return region(self.me, self.kind, self.full, self.axis, (self.me.at(self.axis) + step + 4) % 4, h, self.chunk)

    def push(self, src, dst, n, hop):
        remote(src, dst, self.send, self.recv[n], self.me.ring(self.axis, hop % 4)).start()

    def take(self, n, regions):
        r = ruler(self.measure, self.rows * regions)
        remote(r, r, self.send, self.recv[n], self.me.ring(self.axis, 1)).wait_recv()


class Gather(Phase):
    def copy(self, step, h, n, hop):
        r = self.buf.at[self.idx(step, h)]
        self.push(r, r, n, hop)

    def start(self):
        self.copy(0, None, 0, 1)
        self.copy(0, None, 0, -1)
        if self.small:
            self.copy(0, None, 0, 2)

    def forward(self):
        self.take(0, 2)
        self.copy(-1, 0, 1, 1)
        self.copy(1, 1, 1, -1)

    def finish(self):
        self.take(0, 3) if self.small else self.take(1, 1)


class Scatter(Phase):
    def raw(self, to, step, h, n, hop):
        self.push(self.buf.at[self.idx(step, h)], self.land.at[to], n, hop)

    def start(self):
        if self.small:
            for step in (1, 3, 2):
                for h in range(2):
                    self.raw(2 * (step - 1) + h, step, h, 1, step)
            return
        self.raw(4, 2, 0, 0, 1)
        self.raw(5, 2, 1, 0, -1)
        self.raw(1, 1, 1, 1, 1)
        self.raw(3, -1, 0, 1, -1)

    def forward(self):
        self.take(0, 1)
        for at, step, h, to, hop in ((4, 1, 0, 0, 1), (5, -1, 1, 2, -1)):
            total = self.land[at].astype(F32) + self.buf[self.idx(step, h)].astype(F32)
            self.land[at] = total.astype(BF)
            self.push(self.land.at[at], self.land.at[to], 1, hop)

    def finish(self):
        self.take(1, 3 if self.small else 2)
        for h, slots in ((0, (0, 2, 4) if self.small else (0, 3)), (1, (1, 3, 5) if self.small else (2, 1))):
            total = self.buf[self.idx(0, h)].astype(F32)
            for a in slots:
                total = total + self.land[a].astype(F32)
            if self.final is None:
                self.buf[self.idx(0, h)] = total.astype(BF)
            elif self.kind in MLP:
                self.final[:, :, h * 128:(h + 1) * 128] = total
            else:
                self.final[h] = total


def greet(me):
    bar = pltpu.get_barrier_semaphore()
    x, y, z, c = me.x, me.y, me.z, me.core
    friends = [me.ring("x", s) for s in (1, 2, 3)] + [me.ring("y", s) for s in (1, 2, 3)] + [me.ring("z", s) for s in (1, 2, 3)]
    friends.append(me.dev(core=1 - c))
    for s in range(4):
        zz = (z + s) % 4
        friends.append(me.dev(x=(x + 2) % 4, z=zz, core=1 - c))
        friends.append(me.dev(x=flip(x), z=zz, core=1 - c))
        friends.append(me.dev(y=flip(y), z=zz, core=1 - c))
    friends.append(me.dev(z=flip(z), core=1 - c))
    for f in friends:
        pl.semaphore_signal(bar, inc=1, device_id=f, device_id_type=MESH)
    pl.semaphore_wait(bar, len(friends))


class Route:
    def __init__(self, own, src, dst, send, recv, local, device):
        self.own = own
        self.made_far = lambda: remote(src, dst, send, recv, device)
        self.made_near = lambda: pltpu.make_async_copy(src, dst, local)

    def start(self):
        if self.own is None:
            self.made_far().start()
        else:
            pl.when(self.own)(lambda: self.made_near().start())
            pl.when(jnp.logical_not(self.own))(lambda: self.made_far().start())

    def wait_recv(self):
        if self.own is None:
            self.made_far().wait_recv()
        else:
            pl.when(self.own)(lambda: self.made_near().wait())
            pl.when(jnp.logical_not(self.own))(lambda: self.made_far().wait_recv())

    def wait_send(self):
        if self.own is None:
            self.made_far().wait_send()
        else:
            pl.when(jnp.logical_not(self.own))(lambda: self.made_far().wait_send())


def mapping(me, kind):
    x, y, c = me.x, me.y, me.core
    if kind == "q":
        own = (c + x // 2 + 1) % 2
        return own, dict(x=(x + 2 * (1 - own)) % 4, y=y, core=(c + 1 - own) % 2)
    if kind == "k":
        own = (c + x + 1) % 2
        return own, dict(x=x + (1 - own) * (1 - 2 * (x % 2)), y=y, core=(c + 1 - own) % 2)
    own = (c + y + 1) % 2
    return own, dict(x=x, y=y + (1 - own) * (1 - 2 * (y % 2)), core=(c + 1 - own) % 2)


def lanes_of(z):
    return pl.ds(pl.multiple_of(z * LQ, LQ), LQ)


class Spread:
    def __init__(self, me, wq, wo, wm, bufs, stage, send, recv, local):
        self.me, self.wq, self.wo, self.wm, self.bufs, self.stage = me, wq, wo, wm, bufs, stage
        self.send, self.recv, self.local = send, recv, local

    def qk(self, kind, dz, zsrc, to=None):
        me = self.me
        own, col = mapping(me, kind)
        z = (me.z + dz) % 4
        place = dict(x=me.x, y=me.y) if to is None else col
        dst = self.bufs[kind].at[pick_piece(kind, place["x"], place["y"], z, zsrc)]
        n = zsrc // 2
        return Route((own == 1) & (zsrc == z), self.wq.at[:, lanes_of(z)], dst, self.send.at[dz],
                     self.recv.at[(0 if kind == "q" else 2) + n], self.local.at[0], me.dev(z=z, **col))

    def o(self, dz, zsrc, place):
        me = self.me
        own, col = mapping(me, "o")
        z = (me.z + dz) % 4
        y = me.y if place is None else col["y"]
        dst = self.bufs["o"].at[zsrc % 2, y // 2, me.x, zsrc // 2, y % 2, slice(None), lanes_of(z)]
        return Route((own == 1) & (zsrc == z), self.wo.at[:, lanes_of(z)], dst, self.send.at[4 + dz],
                     self.recv.at[4 + zsrc], self.local.at[1], me.dev(z=z, **col))

    def m(self, dz):
        me = self.me
        z = (me.z + dz) % 4
        return remote(self.wm.at[:, lanes_of(z)], self.stage.at[dz], self.send.at[8 + dz], self.recv.at[8 + dz], me.dev(z=z))

    def start_attention(self):
        me = self.me
        for kind, low in (("q", 0), ("k", 1)):
            @pl.when(me.zlo == low)
            def _(kind=kind):
                for dz in range(4):
                    self.qk(kind, dz, me.z, to=1).start()
        for dz in range(4):
            self.o(dz, me.z, 1).start()

    def start_mlp(self):
        for dz in range(1, 4):
            self.m(dz).start()

    def wait_attention(self):
        for n in range(2):
            self.qk("q", 0, 2 * n).wait_recv()
            self.qk("k", 0, 2 * n + 1).wait_recv()
        for zs in range(4):
            self.o(0, zs, None).wait_recv()

    def wait_mlp(self):
        me = self.me
        for dz in range(1, 4):
            self.m(dz).wait_recv()
        self.stage[0] = self.wm[:, lanes_of(me.z)]
        for t, kind in enumerate("gud"):
            rows = [self.stage[(me.z - zs + 4) % 4, t * 24:(t + 1) * 24, :] for zs in range(4)]
            block = jnp.concatenate(rows, axis=0).astype(BF)
            for j in range(2):
                self.bufs[kind][j, me.x, me.y, :, lanes_of(me.z)] = block[j * 48:(j + 1) * 48]

    def drain(self):
        me = self.me
        for kind, low in (("q", 0), ("k", 1)):
            @pl.when(me.zlo == low)
            def _(kind=kind):
                for dz in range(4):
                    self.qk(kind, dz, me.z, to=1).wait_send()
        for dz in range(4):
            self.o(dz, me.z, 1).wait_send()
        for dz in range(1, 4):
            self.m(dz).wait_send()


def pick_piece(kind, x, y, z, zsrc):
    every = slice(None)
    if kind == "q":
        return (y, x % 2, zsrc // 2, x // 2, every, lanes_of(z))
    return (y, x // 2, zsrc // 2, x % 2, every, lanes_of(z))


class Collect:
    def __init__(self, me, oq, oo, om, finals, send, recv, local):
        self.me, self.oq, self.oo, self.om, self.finals = me, oq, oo, om, finals
        self.send, self.recv, self.local = send, recv, local

    def qk(self, kind, dz):
        me = self.me
        own, col = mapping(me, kind)
        z = (me.z + dz) % 4
        keep = (own == 1) if dz == 0 else None
        return Route(keep, self.finals[kind].at[z // 2], self.oq.at[:, lanes_of(me.z)], self.send.at[dz],
                     self.recv.at[dz], self.local.at[0], me.dev(z=z, **col))

    def o(self, dz):
        me = self.me
        own, col = mapping(me, "o")
        z = (me.z + dz) % 4
        keep = (own == 1) if dz == 0 else None
        return Route(keep, self.finals["o"].at[z % 2, z // 2], self.oo.at[:, lanes_of(me.z)], self.send.at[4 + dz],
                     self.recv.at[4 + dz], self.local.at[1], me.dev(z=z, **col))

    def m(self, t, kind, dz):
        me = self.me
        z = (me.z + dz) % 4
        n = 8 + 4 * t + dz
        src = self.finals[kind].at[z // 2, pl.ds(pl.multiple_of((z % 2) * 24, 8), 24)]
        dst = self.om.at[pl.ds(t * 24, 24), lanes_of(me.z)]
        if dz == 0:
            return pltpu.make_async_copy(src, dst, self.local.at[2 + t])
        return remote(src, dst, self.send.at[n], self.recv.at[n], me.dev(z=z))

    def each_qk(self, act):
        me = self.me
        for dz in range(4):
            for kind, low in (("q", 0), ("k", 1)):
                @pl.when((me.z + dz) % 2 == low)
                def _(kind=kind, dz=dz):
                    act(self.qk(kind, dz))

    def start(self, kind):
        if kind == "qk":
            self.each_qk(lambda r: r.start())
        elif kind == "o":
            for dz in range(4):
                self.o(dz).start()
        else:
            for dz in range(4):
                self.m("gud".index(kind), kind, dz).start()

    def finish(self, kind):
        me = self.me
        if kind == "qk":
            for dz in range(4):
                for k, low in (("q", 0), ("k", 1)):
                    @pl.when(me.zlo == low)
                    def _(k=k, dz=dz):
                        self.qk(k, dz).wait_recv()
            self.each_qk(lambda r: r.wait_send())
        elif kind == "o":
            for dz in range(4):
                self.o(dz).wait_recv()
                self.o(dz).wait_send()
        else:
            for dz in range(4):
                c = self.m("gud".index(kind), kind, dz)
                if dz == 0:
                    c.wait()
                else:
                    c.wait_recv()
                    c.wait_send()


def dot(a, b):
    return jnp.dot(a, b, preferred_element_type=F32)


def dot_t(a, b):
    return lax.dot_general(a, b, (((1,), (1,)), ((), ())), preferred_element_type=F32)


def dot_c(a, b):
    return lax.dot_general(a, b, (((0,), (0,)), ((), ())), preferred_element_type=F32)


def mean_last(v):
    return jnp.mean(v, axis=-1, keepdims=True)


def norm_scale(v):
    return lax.rsqrt(mean_last(v * v) + EPSILON)


def norm_back(dz, v, gain):
    r = norm_scale(v)
    n = v * r
    w = dz * gain
    return r * (w - n * mean_last(w * n)), dz * n


def fold_rows(v):
    return jnp.sum(v.reshape(v.shape[0] // 8, 8, v.shape[1]), axis=0)


def rows_of(i, n):
    return pl.ds(pl.multiple_of(i * n, n), n)


class SmallSum:
    def __init__(self, me, buf, land, send, recv):
        self.me, self.buf, self.land, self.send, self.recv = me, buf, land, send, recv

    def copies(self, stage):
        if stage == 0:
            return [remote(self.buf, self.land.at[0], self.send.at[0], self.recv.at[0], self.me.dev(core=1 - self.me.core))]
        first = 1 + 3 * (stage - 1)
        return [remote(self.buf, self.land.at[first + s], self.send.at[stage], self.recv.at[stage],
                       self.me.ring("xyz"[stage - 1], s + 1)) for s in range(3)]

    def start(self, stage):
        for c in self.copies(stage):
            c.start()

    def finish(self, stage):
        if stage == 0:
            self.copies(0)[0].wait()
            self.buf[...] = self.buf[...] + self.land[0]
        else:
            first = 1 + 3 * (stage - 1)
            three = self.land.at[pl.ds(first, 3)]
            remote(three, three, self.send.at[stage], self.recv.at[stage], self.me.ring("xyz"[stage - 1], 1)).wait()
            self.buf[...] = self.buf[...] + (self.land[first] + self.land[first + 1] + self.land[first + 2])


class Layer:
    def __init__(self, me, S):
        self.me = me
        self.__dict__.update(S)
        c = me.core
        self.mine = rows_of(c, 256)
        self.theirs = rows_of(1 - c, 256)
        self.peer = me.dev(core=1 - c)
        self.wq2 = self.bq.reshape(1024, 1024)
        self.wk2 = self.bk.reshape(1024, 1024)
        self.wo2 = self.bo.reshape(1024, 1024)
        self.mlp = [[S["b" + k].at[j].reshape(768, 1024) for k in "gud"] for j in range(2)]
        self.dq2 = self.tq.reshape(1024, 1024)
        self.dk2 = self.tk.reshape(1024, 1024)
        self.cx, self.mi = self.dq2.at[pl.ds(0, 512)], self.dq2.at[pl.ds(512, 512)]
        self.es = self.dp.at[:, pl.ds(0, 1024)]
        self.lob, self.igb = self.ct.at[pl.ds(0, 256)], self.ct.at[pl.ds(256, 256)]
        self.da, self.dc = self.dk2.at[pl.ds(0, 512)], self.dk2.at[pl.ds(512, 512)]

    def swap(self, n, src, dst):
        me = self.me
        return Route(me.core == me.zlo, src, dst, self.xsend.at[n], self.xrecv.at[n], self.xlocal.at[n],
                     me.dev(z=me.zhi * 2 + me.core, core=me.zlo))

    def share(self, n, src, dst):
        return remote(src, dst, self.xsend.at[n], self.xrecv.at[n], self.peer)

    def tokens_in(self):
        there = self.me.zlo
        return [self.swap(0, self.x_in, self.xa.at[rows_of(there, 256)]),
                self.swap(1, self.seg_in, self.seg.at[there]),
                self.swap(2, self.pos_in, self.pos.at[there]),
                self.swap(3, self.ct_in, self.ct.at[rows_of(there, 256)])]

    def send_piece(self, n, i):
        src, dst = (self.x_in, self.xa) if n == 0 else (self.ct_in, self.ct)
        self.swap(n, src.at[pl.ds(i * 64, 64)], dst.at[pl.ds(pl.multiple_of(self.me.zlo * 256 + i * 64, 64), 64)]).start()

    def tokens_across(self):
        m = self.mine
        c = self.me.core
        return [self.share(4, self.xa.at[m], self.xa.at[m]),
                self.share(5, self.seg.at[c], self.seg.at[c]),
                self.share(6, self.pos.at[c], self.pos.at[c]),
                self.share(7, self.ct.at[m], self.ct.at[m])]

    def gains_rows(self):
        for i in range(8):
            cols = slice(i * 128, (i + 1) * 128)
            self.gv[0:1, cols] = self.ga[i:i + 1, :]
            self.gv[1:2, cols] = self.ga[8 + i:9 + i, :]
        self.gv[2:3, 0:128] = self.ga[16:17, :]
        self.gv[2:3, 128:256] = self.ga[17:18, :]

    def tables(self):
        lane = lax.broadcasted_iota(jnp.int32, (1, 128), 1)
        freqs = jnp.exp((lane % 64).astype(F32) * (-2.0 * math.log(THETA_BASE) / HEAD))
        sign = jnp.where(lane < 64, -1.0, 1.0)
        for h in range(2):
            angle = jnp.broadcast_to(self.pos[h].astype(F32), (128, 256)).T * freqs
            self.cosine[h * 256:(h + 1) * 256] = jnp.cos(angle)
            self.sine[h * 256:(h + 1) * 256] = jnp.sin(angle) * sign
        for q in range(2):
            seg_q = self.seg[q].astype(F32)
            for k in range(q + 1):
                seg_k = jnp.broadcast_to(self.seg[k].astype(F32), (128, 256)).T[:, 0:1]
                key = lax.broadcasted_iota(jnp.int32, (256, 256), 0) + k * 256
                query = lax.broadcasted_iota(jnp.int32, (256, 256), 1) + q * 256
                allowed = (seg_q == seg_k) & (key <= query)
                self.mask[k * 256:(k + 1) * 256, q * 256:(q + 1) * 256] = jnp.where(allowed, 0.0, MASKED).astype(BF)

    def norm_in(self):
        gain = self.gv[0:1, :]

        @pl.loop(0, 8)
        def _(i):
            r = rows_of(i, 64)
            v = self.xa[r].astype(F32)
            self.xn[r] = (v * norm_scale(v) * gain).astype(BF)

    def rope(self, n):
        return n * self.cosine[...] + pltpu.roll(n, 64, 1) * self.sine[...]

    def unrope(self, d, rows):
        return d * self.cosine[rows] - pltpu.roll(d, 64, 1) * self.sine[rows]

    def project(self):
        gq, gk = self.gv[2:3, 0:128], self.gv[2:3, 128:256]

        @pl.loop(0, 4)
        def _(i):
            pre = dot_t(self.xn[...], self.wq2[rows_of(i, 256)])
            for g in range(2):
                v = pre[:, g * 128:(g + 1) * 128]
                cols = pl.ds(pl.multiple_of(i * 256 + g * 128, 128), 128)
                self.qp[:, cols] = v.astype(BF)
                self.qr[:, cols] = self.rope(v * norm_scale(v) * gq).astype(BF)

        @pl.loop(0, 2)
        def _(i):
            pre = dot_t(self.xn[...], self.wk2[rows_of(i, 256)])
            for g in range(2):
                v = pre[:, g * 128:(g + 1) * 128]
                cols = pl.ds(pl.multiple_of(i * 256 + g * 128, 128), 128)
                self.kp[:, cols] = v.astype(BF)
                self.kr[:, cols] = self.rope(v * norm_scale(v) * gk).astype(BF)
            self.vl[:, rows_of(i, 256)] = dot_t(self.xn[...], self.wk2[rows_of(i + 2, 256)]).astype(BF)

    def attend(self):
        factor = HEAD ** -0.5 * 1.4426950408889634

        @pl.loop(0, 4)
        def _(k):
            kcols = rows_of(k, 128)
            for b in range(2):
                n = 256 * (b + 1)
                rows = slice(b * 256, (b + 1) * 256)
                keys, values = self.kr[0:n, kcols], self.vl[0:n, kcols]
                for g in range(2):
                    qcols = pl.ds(pl.multiple_of(k * 256 + g * 128, 128), 128)
                    s = dot_t(keys, self.qr[rows, qcols])
                    p = jnp.exp2(s * factor + self.mask[0:n, rows].astype(F32))
                    p = (p * (1.0 / jnp.sum(p, axis=0, keepdims=True))).astype(BF)
                    (self.p0 if b == 0 else self.p1)[2 * k + g] = p
                    self.cx[rows, qcols] = dot_c(values, p).T.astype(BF)

    def exchange(self, n, chunk, land):
        cols = slice(chunk * 256, (chunk + 1) * 256)
        return self.share(n + chunk, self.es.at[:, cols], land.at[:, cols])

    def out_project(self):
        for j in range(4):
            cols = slice(j * 256, (j + 1) * 256)
            part = dot(self.cx[...], self.wo2[:, cols])
            self.es[:, cols] = part.astype(BF)
            self.exchange(8, j, self.r0).start()
            self.hid[:, cols] = part + self.xa[:, cols].astype(F32)

    def norm_mid(self):
        for j in range(4):
            self.exchange(8, j, self.r0).wait()
        gain = self.gv[1:2, :]

        @pl.loop(0, 8)
        def _(i):
            r = rows_of(i, 64)
            v = self.hid[r] + self.r0[r].astype(F32)
            self.hid[r] = v
            self.mi[r] = (v * norm_scale(v) * gain).astype(BF)

    def units(self, j, c):
        wg2, wu2, wd2 = self.mlp[j]
        r = rows_of(c, 256)
        gate = dot_t(self.mi[...], wg2[r])
        up = dot_t(self.mi[...], wu2[r])
        back = dot_t(self.ct[...], wd2[r])
        sig = jax.nn.sigmoid(gate)
        silu = gate * sig
        act = (silu * up).astype(BF)
        d_gate = (back * up * sig * (1.0 + gate * (1.0 - sig))).astype(BF)
        d_up = (back * silu).astype(BF)
        self.acc_d[...] += dot(d_gate, wg2[r]) + dot(d_up, wu2[r])
        return act, d_gate, d_up

    def unit_grads(self, j, c, act, d_gate, d_up):
        wg2, wu2, wd2 = self.mlp[j]
        r = rows_of(c, 256)
        self.acc_o[...] += dot(act, wd2[r])
        wd2[r] = dot_c(act, self.ct[...]).astype(BF)
        wg2[r] = dot_c(d_gate, self.mi[...]).astype(BF)
        wu2[r] = dot_c(d_up, self.mi[...]).astype(BF)

    def held_units(self, c):
        cols = rows_of(c, 256)
        upper = pl.ds(pl.multiple_of(1024 + c * 256, 256), 256)
        return self.da.at[:, cols], self.dc.at[:, cols], self.dp.at[:, upper]

    def feed_forward(self, j, c):
        self.unit_grads(j, c, *self.units(j, c))

    def feed_forward_first(self, c):
        for ref, v in zip(self.held_units(c), self.units(1, c)):
            ref[...] = v

    def feed_forward_rest(self, c):
        self.unit_grads(1, c, *(ref[...] for ref in self.held_units(c)))

    def send_mid(self):
        for j in range(4):
            cols = slice(j * 256, (j + 1) * 256)
            self.es[:, cols] = self.acc_d[:, cols].astype(BF)
            self.exchange(12, j, self.r1).start()

    def norm_mid_back(self):
        for j in range(4):
            self.exchange(12, j, self.r1).wait()
        gain = self.gv[1:2, :]

        def body(i, total):
            r = rows_of(i, 64)
            dz = self.acc_d[r] + self.r1[r].astype(F32)
            dv, term = norm_back(dz, self.hid[r], gain)
            d = self.ct[r].astype(F32) + dv
            self.acc_d[r] = d
            self.da[r] = d.astype(BF)
            return total + fold_rows(term) * (i // 4 == self.me.core).astype(F32)

        total = lax.fori_loop(0, 8, body, jnp.zeros((8, 1024), F32))
        self.gg[1:2, :] = jnp.sum(total, axis=0, keepdims=True)

    def send_output(self):
        self.ls[...] = self.acc_o[self.theirs].astype(BF)
        self.share(16, self.ls, self.r0.at[pl.ds(0, 256)]).start()

    def finish_output(self):
        self.share(16, self.ls, self.r0.at[pl.ds(0, 256)]).wait()
        self.lob[...] = (self.acc_o[self.mine] + self.hid[self.mine] + self.r0[0:256].astype(F32)).astype(BF)

    def out_back(self):
        for j in range(4):
            r = slice(j * 256, (j + 1) * 256)
            self.dc[:, r] = dot_t(self.da[...], self.wo2[r]).astype(BF)

    def attend_back(self, between):
        scale = HEAD ** -0.5
        gq, gk = self.gv[2:3, 0:128], self.gv[2:3, 128:256]

        def body(k, totals):
            total_q, total_k = totals
            r = rows_of(k, 256)
            self.wo2[r] = dot_c(self.cx[:, r], self.da[...]).astype(BF)
            kcols = rows_of(k, 128)
            dk, dv = [0.0, 0.0], [0.0, 0.0]
            for b in range(2):
                n = 256 * (b + 1)
                rows = slice(b * 256, (b + 1) * 256)
                keys, values = self.kr[0:n, kcols], self.vl[0:n, kcols]
                for g in range(2):
                    qcols = pl.ds(pl.multiple_of(k * 256 + g * 128, 128), 128)
                    low = (self.p0 if b == 0 else self.p1)[2 * k + g]
                    dc = self.dc[rows, qcols]
                    p = low.astype(F32)
                    t = p * dot_t(values, dc)
                    ds = (t - p * jnp.sum(t, axis=0, keepdims=True)).astype(BF)
                    dz = self.unrope(dot_c(keys, ds).T * scale, rows)
                    dq, term = norm_back(dz, self.qp[rows, qcols].astype(F32), gq)
                    self.dp[rows, qcols] = dq.astype(BF)
                    total_q = total_q + fold_rows(term)
                    pk, pv = dot(ds, self.qr[rows, qcols]), dot(low, dc)
                    for j in range(b + 1):
                        part = slice(j * 256, (j + 1) * 256)
                        dk[j] = dk[j] + pk[part]
                        dv[j] = dv[j] + pv[part]
            for j in range(2):
                rows = slice(j * 256, (j + 1) * 256)
                dz = self.unrope(dk[j] * scale, rows)
                dkey, term = norm_back(dz, self.kp[rows, kcols].astype(F32), gk)
                self.dp[rows, pl.ds(pl.multiple_of(1024 + k * 128, 128), 128)] = dkey.astype(BF)
                self.dp[rows, pl.ds(pl.multiple_of(1536 + k * 128, 128), 128)] = dv[j].astype(BF)
                total_k = total_k + fold_rows(term)
            between(k)
            return total_q, total_k

        zero = jnp.zeros((8, 128), F32)
        total_q, total_k = lax.fori_loop(0, 4, body, (zero, zero))
        self.gg[2:3, 0:128] = jnp.sum(total_q, axis=0, keepdims=True)
        self.gg[2:3, 128:256] = jnp.sum(total_k, axis=0, keepdims=True)

    def project_back(self, kind):
        grad, first = (self.dq2, 0) if kind == "q" else (self.dk2, 1024)

        @pl.loop(0, 4)
        def _(j):
            cols = pl.ds(pl.multiple_of(first + j * 256, 256), 256)
            grad[rows_of(j, 256)] = dot_c(self.dp[:, cols], self.xn[...]).astype(BF)

    def d_normed(self, rows):
        return dot(self.dp[rows, 0:1024], self.wq2[...]) + dot(self.dp[rows, 1024:2048], self.wk2[...])

    def send_in(self):
        self.ls[...] = self.d_normed(self.theirs).astype(BF)
        self.share(18, self.ls, self.r0.at[pl.ds(256, 256)]).start()

    def finish_input(self):
        self.hid[0:256] = self.d_normed(self.mine)
        self.share(18, self.ls, self.r0.at[pl.ds(256, 256)]).wait()
        gain = self.gv[0:1, :]

        def body(i, total):
            r = rows_of(i, 64)
            at = pl.ds(pl.multiple_of(self.me.core * 256 + i * 64, 64), 64)
            over = pl.ds(pl.multiple_of(256 + i * 64, 64), 64)
            dz = self.hid[r] + self.r0[over].astype(F32)
            dv, term = norm_back(dz, self.xa[at].astype(F32), gain)
            self.igb[r] = (self.acc_d[at] + dv).astype(BF)
            return total + fold_rows(term)

        total = lax.fori_loop(0, 4, body, jnp.zeros((8, 1024), F32))
        self.gg[0:1, :] = jnp.sum(total, axis=0, keepdims=True)

    def gains_flat(self):
        for i in range(8):
            cols = slice(i * 128, (i + 1) * 128)
            self.gs[i:i + 1, :] = self.gg[0:1, cols]
            self.gs[8 + i:9 + i, :] = self.gg[1:2, cols]
        self.gs[16:17, :] = self.gg[2:3, 0:128]
        self.gs[17:18, :] = self.gg[2:3, 128:256]
        self.gs[18:24, :] = jnp.zeros((6, 128), F32)


INPUTS = ("x_in", "ct_in", "seg_in", "pos_in", "wq_in", "wo_in", "wm_in", "gain_in")
OUTPUTS = ("lo", "ig", "oq", "oo", "om", "gs")
V, SEM = pltpu.VMEM, pltpu.SemaphoreType.DMA


def scratch():
    s = {"b" + k: V(SHAPES[k], BF) for k in KINDS}
    s.update(tq=V(SHAPES["q"], BF), tk=V(SHAPES["k"], BF))
    s.update(stage=V((4, 72, 256), F32), wqt=V((32, 1024), BF), wov=V((16, 1024), BF), wmv=V((3, 24, 1024), BF), wmf=V((72, 1024), F32))
    s.update(xa=V((512, 1024), BF), ct=V((512, 1024), BF), seg=V((2, 1, 256), jnp.int32), pos=V((2, 1, 256), jnp.int32), xn=V((512, 1024), BF))
    s.update(qp=V((512, 1024), BF), kp=V((512, 512), BF), qr=V((512, 1024), BF), kr=V((512, 512), BF), vl=V((512, 512), BF))
    s.update(cosine=V((512, 128), F32), sine=V((512, 128), F32), mask=V((512, 512), BF))
    s.update(p0=V((8, 256, 256), BF), p1=V((8, 512, 256), BF))
    s.update(hid=V((512, 1024), F32), acc_o=V((512, 1024), F32), acc_d=V((512, 1024), F32))
    s.update(r0=V((512, 1024), BF), r1=V((512, 1024), BF))
    s.update(ls=V((256, 1024), BF))
    s.update(dp=V((512, 2048), BF))
    s.update(ga=V((24, 128), F32), gv=V((8, 1024), F32), gg=V((8, 1024), F32), land_a=V((10, 24, 128), F32), land_b=V((10, 24, 128), F32))
    for k in KINDS:
        order = ORDERS[k]
        for n, (p, chunk) in enumerate(PHASES[k]):
            s["land_%s%d" % (k, n)] = V((6,) + half_shape(k, order[:p], order[p], chunk), BF)
    for k in "qkogud":
        s["final_" + k] = V({"q": (2, 32, 256), "k": (2, 32, 256), "o": (2, 2, 16, 256)}.get(k, (2, 48, 256)), F32)
    phases = 2 * sum(len(p) for p in PHASES.values())
    for name, n in (("spread", 12), ("collect", 20), ("small_a", 4), ("small_b", 4)):
        s[name + "_send"], s[name + "_recv"] = SEM((n,)), SEM((n,))
    s.update(gather_recv=SEM((phases,)), scatter_recv=SEM((phases,)))
    s.update(spread_local=SEM((2,)), collect_local=SEM((5,)), xsend=SEM((20,)), xrecv=SEM((20,)), xlocal=SEM((20,)), drained=SEM((4 * len(KINDS),)), fetch=SEM((3,)))
    return s


def kernel(*refs):
    shapes = scratch()
    S = dict(zip(INPUTS + OUTPUTS + tuple(shapes), refs))
    me = Place()
    fetch = [pltpu.make_async_copy(S[a], S[b], S["fetch"].at[n]) for n, (a, b) in
             enumerate((("wq_in", "wqt"), ("wo_in", "wov"), ("wm_in", "wmv")))]
    for c in fetch:
        c.start()
    greet(me)
    L = Layer(me, S)
    bufs = {k: S["b" + k] for k in KINDS}
    grads = dict(bufs, q=S["tq"], k=S["tk"])
    finals = {k: S["final_" + k] for k in "qkogud"}
    sp = Spread(me, S["wqt"], S["wov"], S["wmf"], bufs, S["stage"], S["spread_send"], S["spread_recv"], S["spread_local"])
    ga = SmallSum(me, S["ga"], S["land_a"], S["small_a_send"], S["small_a_recv"])
    gb = SmallSum(me, S["gs"], S["land_b"], S["small_b_send"], S["small_b_recv"])
    C = Collect(me, S["oq"], S["oo"], S["om"], finals, S["collect_send"], S["collect_recv"], S["collect_local"])
    gathers, scatters, sent, n = {}, {}, S["drained"], 0
    measure = S["bg"].reshape(1536, 1024)
    for i, k in enumerate(KINDS):
        for j, (p, chunk) in enumerate(PHASES[k]):
            two = lambda name: (S[name].at[2 * n], S[name].at[2 * n + 1])
            gathers[k, p, chunk] = Gather(me, k, p, chunk, bufs[k], None, measure, sent.at[2 * i + (chunk == 1)], two("gather_recv"))
            scatters[k, p, chunk] = Scatter(me, k, p, chunk, grads[k], S["land_%s%d" % (k, j)], measure,
                                            sent.at[12 + 2 * i + (chunk is not None)], two("scatter_recv"), finals[k] if p == 0 else None)
            n += 1

    def drain(sem, rows):
        r = ruler(measure, rows)
        remote(r, r, sem, S["gather_recv"].at[0], me.ring("x", 1)).wait_send()

    def run(table, kinds, p, chunk, acts):
        for act in acts:
            for k in kinds:
                getattr(table[k, p, chunk], act)()

    def G(kinds, p, *acts, chunk=None):
        run(gathers, kinds, p, chunk, acts)

    def R(kinds, p, *acts, chunk=None):
        run(scatters, kinds, p, chunk, acts)

    arrive = L.tokens_in()
    across = L.tokens_across()
    fetch[0].wait()
    fetch[1].wait()
    sp.start_attention()
    arrive[1].start()
    arrive[2].start()
    L.send_piece(0, 0)
    L.send_piece(0, 1)
    first = 18 * (me.zlo * 64 + me.dp)
    wide = jnp.concatenate([S["gain_in"][...].astype(F32), jnp.zeros((1, 238), F32)], axis=1)
    wide = pltpu.roll(jnp.broadcast_to(wide, (8, 256)), first % 128, 1)[0:1]
    S["ga"][...] = jnp.zeros((24, 128), F32)
    S["ga"][pl.ds(first // 128, 1), :] = wide[:, 0:128]
    S["ga"][pl.ds(first // 128 + 1, 1), :] = wide[:, 128:256]
    ga.start(0)
    fetch[2].wait()
    for t in range(3):
        S["wmf"][t * 24:(t + 1) * 24, :] = S["wmv"][t].astype(F32)
    sp.wait_attention()
    G(ATT, 0, "start")
    sp.start_mlp()
    ga.finish(0)
    ga.start(1)
    L.send_piece(0, 2)
    L.send_piece(0, 3)
    sp.wait_mlp()
    G(MLP, 0, "start")
    G(ATT, 0, "finish")
    G(ATT, 1, "start")
    L.send_piece(3, 0)
    ga.finish(1)
    ga.start(2)
    L.acc_o[...] = jnp.zeros((512, 1024), F32)
    L.acc_d[...] = jnp.zeros((512, 1024), F32)
    G(MLP, 0, "finish")
    G(MLP, 1, "start")
    G(ATT, 1, "forward")
    ga.finish(2)
    ga.start(3)
    for c in arrive[:3]:
        c.wait_recv()
    for c in across[:3]:
        c.start()
    G(ATT, 1, "finish")
    G(ATT, 2, "start")
    G(MLP, 1, "forward")
    ga.finish(3)
    L.gains_rows()
    for c in across[:3]:
        c.wait()
    L.tables()
    L.norm_in()
    G(ATT, 2, "forward")
    G(MLP, 1, "finish")
    G(MLP, 2, "start", chunk=0)
    for i in range(1, 4):
        L.send_piece(3, i)
    G(MLP, 2, "start", chunk=1)
    G(ATT, 2, "finish")
    L.project()
    G(MLP, 2, "forward", chunk=0)
    L.attend()
    arrive[3].wait_recv()
    across[3].start()
    L.out_project()
    across[3].wait()
    for c in arrive:
        c.wait_send()
    sp.drain()
    L.norm_mid()
    G(MLP, 2, "finish", chunk=0)
    for i, k in enumerate(KINDS):
        drain(sent.at[2 * i], 63 * 16 if k in ATT else 3 * 24 + 12 * 24 + 48 * 12)

    @pl.loop(0, 3)
    def _(c):
        L.feed_forward(0, c)

        @pl.when(c == 0)
        def _():
            G(MLP, 2, "forward", chunk=1)

    R(MLP, 2, "start", chunk=0)
    G(MLP, 2, "finish", chunk=1)
    for i in range(3, 6):
        drain(sent.at[2 * i + 1], 48 * 12)

    @pl.loop(0, 3)
    def _(c):
        L.feed_forward_first(c)

    L.send_mid()
    R(MLP, 2, "forward", chunk=0)
    pl.loop(0, 3)(L.feed_forward_rest)
    R(MLP, 2, "start", chunk=1)
    L.norm_mid_back()
    L.send_output()
    R(MLP, 2, "finish", chunk=0)
    L.out_back()
    R(MLP, 2, "forward", chunk=1)

    def between(k):
        @pl.when(k == 0)
        def _():
            L.finish_output()
            L.swap(17, L.lob, L.lo).start()

        @pl.when(k == 2)
        def _():
            R(MLP, 2, "finish", chunk=1)
            R(MLP, 1, "start")

    L.attend_back(between)
    R("o", 2, "start")
    L.project_back("q")
    R("q", 2, "start")
    R(MLP, 1, "forward")
    L.project_back("k")
    R("k", 2, "start")
    L.send_in()
    R("o", 2, "forward")
    R("q", 2, "forward")
    L.finish_input()
    R("k", 2, "forward")
    L.gains_flat()
    gb.start(0)
    R(MLP, 1, "finish")
    R(MLP, 0, "start")
    gb.finish(0)
    gb.start(1)
    R("o", 2, "finish")
    R("o", 1, "start")
    R("q", 2, "finish")
    R("q", 1, "start")
    R("k", 2, "finish")
    R("k", 1, "start")
    R(MLP, 0, "finish")
    for k in MLP:
        C.start(k)
    gb.finish(1)
    gb.start(2)
    R("o", 1, "forward")
    R("q", 1, "forward")
    R("k", 1, "forward")
    L.swap(19, L.igb, L.ig).start()
    gb.finish(2)
    gb.start(3)
    R("o", 1, "finish")
    R("o", 0, "start")
    R("q", 1, "finish")
    R("q", 0, "start")
    R("k", 1, "finish")
    R("k", 0, "start")
    R("o", 0, "finish")
    C.start("o")
    R("qk", 0, "finish")
    C.start("qk")
    gb.finish(3)
    for k in ("g", "u", "d", "o", "qk"):
        C.finish(k)
    for i, k in enumerate(KINDS):
        if k in ATT:
            drain(sent.at[12 + 2 * i], 63 * 16)
        else:
            drain(sent.at[12 + 2 * i], 15 * 24)
            drain(sent.at[13 + 2 * i], 96 * 12)
    for n, src, dst in ((17, L.lob, L.lo), (19, L.igb, L.ig)):
        c = L.swap(n, src, dst)
        c.wait_recv()
        c.wait_send()


def finish_kernel(*refs):
    given, gs, outs, gain_out, held, sem = refs[:5], refs[5], refs[6:11], refs[11], refs[12:17], refs[17]
    loads = [pltpu.make_async_copy(a, b, sem.at[n]) for n, (a, b) in enumerate(zip(given, held))]
    stores = [pltpu.make_async_copy(a, b, sem.at[5 + n]) for n, (a, b) in enumerate(zip(held, outs))]
    for m in loads:
        m.start()
    first = 18 * (lax.axis_index("seq") * 64 + lax.axis_index("dp"))
    wide = jnp.concatenate([gs[pl.ds(first // 128, 1), :], gs[pl.ds(first // 128 + 1, 1), :]], axis=1)
    wide = pltpu.roll(jnp.broadcast_to(wide, (8, 256)), 256 - first % 128, 1)
    gain_out[...] = wide[0:1, 0:18]
    for load, store in zip(loads, stores):
        load.wait()
        store.start()
    for m in stores:
        m.wait()


def shards(layer_input, segments, positions, qkv_weight, out_weight, mlp_weight, gains, cotangent):
    vm, hbm = pl.BlockSpec(memory_space=pltpu.VMEM), pl.BlockSpec(memory_space=pl.ANY)
    shape = jax.ShapeDtypeStruct
    lo, ig, oq, oo, om, gs = pl.pallas_call(
        kernel,
        out_shape=(shape((256, 1024), BF), shape((256, 1024), BF), shape((32, 1024), F32), shape((16, 1024), F32),
                   shape((72, 1024), F32), shape((24, 128), F32)),
        in_specs=[hbm] * 7 + [vm],
        out_specs=(hbm,) * 5 + (vm,),
        scratch_shapes=list(scratch().values()),
        compiler_params=pltpu.CompilerParams(collective_id=0, has_side_effects=True, vmem_limit_bytes=VMEM_BYTES),
    )(layer_input[0], cotangent[0], segments, positions, qkv_weight.T, out_weight, jnp.transpose(mlp_weight, (1, 0, 2)), gains.reshape(1, 18))
    lo, ig, oq, oo, om, gs = pl.pallas_call(
        finish_kernel,
        out_shape=(shape((256, 1024), BF), shape((256, 1024), BF), shape((32, 1024), F32), shape((16, 1024), F32),
                   shape((72, 1024), F32), shape((1, 18), F32)),
        in_specs=[hbm] * 5 + [vm],
        out_specs=(hbm,) * 5 + (vm,),
        scratch_shapes=[V((256, 1024), BF), V((256, 1024), BF), V((32, 1024), F32), V((16, 1024), F32), V((72, 1024), F32), SEM((10,))],
    )(lo, ig, oq, oo, om, gs)
    return lo[None], ig[None], oq.T, oo, jnp.transpose(om.reshape(3, 24, 1024), (1, 0, 2)), gs.reshape(18)


def solution(mesh):
    rows, split = P("dp", "seq", None), ("seq", "dp")
    weights = (P(None, split), P(split, None), P(split, None, None), P(split))
    return jax.shard_map(shards, mesh=mesh, in_specs=(rows, P("dp", "seq"), P("dp", "seq")) + weights + (rows,),
                         out_specs=(rows, rows) + weights, check_vma=False)
```

```python
import math
import jax, jax.numpy as jnp
from jax import lax
from jax.experimental import pallas as pl
from jax.experimental.pallas import tpu as pltpu
from jax.sharding import PartitionSpec as P

MESH = pl.DeviceIdType.MESH
BF = jnp.bfloat16
F32 = jnp.float32
LQ = 256
HEAD = 128
EPSILON = 1e-06
THETA_BASE = 1000000.0
MASKED = -1e30
VMEM_BYTES = 63 << 20
SHAPES = {"q": (4, 2, 2, 2, 32, 1024), "k": (4, 2, 2, 2, 32, 1024), "o": (2, 2, 4, 2, 2, 16, 1024),
          **{k: (2, 4, 4, 48, 1024) for k in "gud"}}
ORDERS = {"q": "xyz", "k": "yzx", "o": "zxy", "g": "xyz", "u": "yzx", "d": "zxy"}
KINDS = "qkogud"
ATT, MLP = "qko", "gud"
PHASES = {k: [(0, None), (1, None)] + ([(2, 0), (2, 1)] if k in "gud" else [(2, None)]) for k in KINDS}


def pick(kind, x, y, z, h, chunk):
    every = slice(None)
    at = lambda v: every if v is None else v
    low = lambda v: every if v is None else v % 2
    high = lambda v: every if v is None else v // 2
    lanes = every if z is None else pl.ds(pl.multiple_of(z * LQ, LQ), LQ)
    if kind == "q":
        return (at(y), low(x), at(h), high(x), every, lanes)
    if kind == "k":
        return (at(y), high(x), at(h), low(x), every, lanes)
    if kind == "o":
        return (at(h), high(y), at(x), every, low(y), every, lanes)
    if h is not None:
        lanes = pl.ds(h * 512, 512) if z is None else pl.ds(pl.multiple_of(z * LQ + h * 128, 128), 128)
    return (at(chunk), at(x), at(y), every, lanes)


def half_shape(kind, full, axis, chunk):
    n = lambda a: 4 if a in full else None
    x, y, z = n("x"), n("y"), n("z")
    lanes = 1024 if z else 256
    if kind in "qk":
        s = ([4] if y else []) + ([2, 2] if x else []) + [32, lanes]
    elif kind == "o":
        s = ([2] if y else []) + ([4] if x else []) + [2] + ([2] if y else []) + [16, lanes]
    else:
        s = ([2] if chunk is None else []) + ([4] if x else []) + ([4] if y else []) + [48, lanes // 2]
    return tuple(s)


class Place:
    def __init__(self):
        s, d = lax.axis_index("seq"), lax.axis_index("dp")
        self.zlo, self.dp = s, d
        self.core = d % 2
        self.zhi = (d // 2) % 2
        self.x = (d // 4) % 4
        self.y = d // 16
        self.z = self.zhi * 2 + s

    def dev(self, x=None, y=None, z=None, core=None):
        x = self.x if x is None else x
        y = self.y if y is None else y
        z = self.z if z is None else z
        core = self.core if core is None else core
        return (z % 2, ((y * 4 + x) * 2 + z // 2) * 2 + core)

    def at(self, axis):
        return {"x": self.x, "y": self.y, "z": self.z}[axis]

    def ring(self, axis, step):
        return self.dev(**{axis: (self.at(axis) + step) % 4})


def flip(v):
    return v + 1 - 2 * (v % 2)


def block_rows(kind, phase, chunk):
    return 4 ** phase * (16 if kind in ATT else 24 if chunk is None else 12)


def ruler(ref, rows):
    for lanes in (1024, 768, 512, 256):
        n = rows * 1024 // lanes
        if rows * 1024 % lanes == 0 and n % 16 == 0 and n <= ref.shape[0]:
            return ref.at[pl.ds(0, n), pl.ds(0, lanes)]
    raise ValueError(rows)


def region(me, kind, full, axis, val, h=None, chunk=None):
    c = {a: (None if a in full else me.at(a)) for a in "xyz"}
    c[axis] = val
    return pick(kind, c["x"], c["y"], c["z"], h, chunk)


def remote(src, dst, send, recv, device):
    return pltpu.make_async_remote_copy(src_ref=src, dst_ref=dst, send_sem=send, recv_sem=recv, device_id=device, device_id_type=MESH)


class Phase:
    def __init__(self, me, kind, phase, chunk, buf, land, measure, send, recv, final=None):
        self.me, self.kind, self.chunk, self.buf, self.land, self.measure = me, kind, chunk, buf, land, measure
        self.send, self.recv, self.final = send, recv, final
        order = ORDERS[kind]
        self.axis, self.full = order[phase], order[:phase]
        self.rows = block_rows(kind, phase, chunk)
        self.small = phase == 0

    def idx(self, step, h=None):
        return region(self.me, self.kind, self.full, self.axis, (self.me.at(self.axis) + step + 4) % 4, h, self.chunk)

    def push(self, src, dst, n, hop):
        remote(src, dst, self.send, self.recv[n], self.me.ring(self.axis, hop % 4)).start()

    def take(self, n, regions):
        r = ruler(self.measure, self.rows * regions)
        remote(r, r, self.send, self.recv[n], self.me.ring(self.axis, 1)).wait_recv()


class Gather(Phase):
    def copy(self, step, h, n, hop):
        r = self.buf.at[self.idx(step, h)]
        self.push(r, r, n, hop)

    def start(self):
        self.copy(0, None, 0, 1)
        self.copy(0, None, 0, -1)
        if self.small:
            self.copy(0, None, 0, 2)

    def forward(self):
        self.take(0, 2)
        self.copy(-1, 0, 1, 1)
        self.copy(1, 1, 1, -1)

    def finish(self):
        self.take(0, 3) if self.small else self.take(1, 1)


class Scatter(Phase):
    def raw(self, to, step, h, n, hop):
        self.push(self.buf.at[self.idx(step, h)], self.land.at[to], n, hop)

    def start(self):
        if self.small:
            for step in (1, 3, 2):
                for h in range(2):
                    self.raw(2 * (step - 1) + h, step, h, 1, step)
            return
        self.raw(4, 2, 0, 0, 1)
        self.raw(5, 2, 1, 0, -1)
        self.raw(1, 1, 1, 1, 1)
        self.raw(3, -1, 0, 1, -1)

    def forward(self):
        self.take(0, 1)
        for at, step, h, to, hop in ((4, 1, 0, 0, 1), (5, -1, 1, 2, -1)):
            total = self.land[at].astype(F32) + self.buf[self.idx(step, h)].astype(F32)
            self.land[at] = total.astype(BF)
            self.push(self.land.at[at], self.land.at[to], 1, hop)

    def finish(self):
        self.take(1, 3 if self.small else 2)
        for h, slots in ((0, (0, 2, 4) if self.small else (0, 3)), (1, (1, 3, 5) if self.small else (2, 1))):
            total = self.buf[self.idx(0, h)].astype(F32)
            for a in slots:
                total = total + self.land[a].astype(F32)
            if self.final is None:
                self.buf[self.idx(0, h)] = total.astype(BF)
            elif self.kind in MLP:
                self.final[:, :, h * 128:(h + 1) * 128] = total
            else:
                self.final[h] = total


def greet(me):
    bar = pltpu.get_barrier_semaphore()
    x, y, z, c = me.x, me.y, me.z, me.core
    friends = [me.ring("x", s) for s in (1, 2, 3)] + [me.ring("y", s) for s in (1, 2, 3)] + [me.ring("z", s) for s in (1, 2, 3)]
    friends.append(me.dev(core=1 - c))
    for s in range(4):
        zz = (z + s) % 4
        friends.append(me.dev(x=(x + 2) % 4, z=zz, core=1 - c))
        friends.append(me.dev(x=flip(x), z=zz, core=1 - c))
        friends.append(me.dev(y=flip(y), z=zz, core=1 - c))
    friends.append(me.dev(z=flip(z), core=1 - c))
    for f in friends:
        pl.semaphore_signal(bar, inc=1, device_id=f, device_id_type=MESH)
    pl.semaphore_wait(bar, len(friends))


class Route:
    def __init__(self, own, src, dst, send, recv, local, device):
        self.own = own
        self.made_far = lambda: remote(src, dst, send, recv, device)
        self.made_near = lambda: pltpu.make_async_copy(src, dst, local)

    def start(self):
        if self.own is None:
            self.made_far().start()
        else:
            pl.when(self.own)(lambda: self.made_near().start())
            pl.when(jnp.logical_not(self.own))(lambda: self.made_far().start())

    def wait_recv(self):
        if self.own is None:
            self.made_far().wait_recv()
        else:
            pl.when(self.own)(lambda: self.made_near().wait())
            pl.when(jnp.logical_not(self.own))(lambda: self.made_far().wait_recv())

    def wait_send(self):
        if self.own is None:
            self.made_far().wait_send()
        else:
            pl.when(jnp.logical_not(self.own))(lambda: self.made_far().wait_send())


def mapping(me, kind):
    x, y, c = me.x, me.y, me.core
    if kind == "q":
        own = (c + x // 2 + 1) % 2
        return own, dict(x=(x + 2 * (1 - own)) % 4, y=y, core=(c + 1 - own) % 2)
    if kind == "k":
        own = (c + x + 1) % 2
        return own, dict(x=x + (1 - own) * (1 - 2 * (x % 2)), y=y, core=(c + 1 - own) % 2)
    own = (c + y + 1) % 2
    return own, dict(x=x, y=y + (1 - own) * (1 - 2 * (y % 2)), core=(c + 1 - own) % 2)


def lanes_of(z):
    return pl.ds(pl.multiple_of(z * LQ, LQ), LQ)


class Spread:
    def __init__(self, me, wq, wo, wm, bufs, stage, send, recv, local):
        self.me, self.wq, self.wo, self.wm, self.bufs, self.stage = me, wq, wo, wm, bufs, stage
        self.send, self.recv, self.local = send, recv, local

    def qk(self, kind, dz, zsrc, to=None):
        me = self.me
        own, col = mapping(me, kind)
        z = (me.z + dz) % 4
        place = dict(x=me.x, y=me.y) if to is None else col
        dst = self.bufs[kind].at[pick_piece(kind, place["x"], place["y"], z, zsrc)]
        n = zsrc // 2
        return Route((own == 1) & (zsrc == z), self.wq.at[:, lanes_of(z)], dst, self.send.at[dz],
                     self.recv.at[(0 if kind == "q" else 2) + n], self.local.at[0], me.dev(z=z, **col))

    def o(self, dz, zsrc, place):
        me = self.me
        own, col = mapping(me, "o")
        z = (me.z + dz) % 4
        y = me.y if place is None else col["y"]
        dst = self.bufs["o"].at[zsrc % 2, y // 2, me.x, zsrc // 2, y % 2, slice(None), lanes_of(z)]
        return Route((own == 1) & (zsrc == z), self.wo.at[:, lanes_of(z)], dst, self.send.at[4 + dz],
                     self.recv.at[4 + zsrc], self.local.at[1], me.dev(z=z, **col))

    def m(self, dz):
        me = self.me
        z = (me.z + dz) % 4
        return remote(self.wm.at[:, lanes_of(z)], self.stage.at[dz], self.send.at[8 + dz], self.recv.at[8 + dz], me.dev(z=z))

    def start_attention(self):
        me = self.me
        for kind, low in (("q", 0), ("k", 1)):
            @pl.when(me.zlo == low)
            def _(kind=kind):
                for dz in range(4):
                    self.qk(kind, dz, me.z, to=1).start()
        for dz in range(4):
            self.o(dz, me.z, 1).start()

    def start_mlp(self):
        for dz in range(1, 4):
            self.m(dz).start()

    def wait_attention(self):
        for n in range(2):
            self.qk("q", 0, 2 * n).wait_recv()
            self.qk("k", 0, 2 * n + 1).wait_recv()
        for zs in range(4):
            self.o(0, zs, None).wait_recv()

    def wait_mlp(self):
        me = self.me
        for dz in range(1, 4):
            self.m(dz).wait_recv()
        self.stage[0] = self.wm[:, lanes_of(me.z)]
        for t, kind in enumerate("gud"):
            rows = [self.stage[(me.z - zs + 4) % 4, t * 24:(t + 1) * 24, :] for zs in range(4)]
            block = jnp.concatenate(rows, axis=0).astype(BF)
            for j in range(2):
                self.bufs[kind][j, me.x, me.y, :, lanes_of(me.z)] = block[j * 48:(j + 1) * 48]

    def drain(self):
        me = self.me
        for kind, low in (("q", 0), ("k", 1)):
            @pl.when(me.zlo == low)
            def _(kind=kind):
                for dz in range(4):
                    self.qk(kind, dz, me.z, to=1).wait_send()
        for dz in range(4):
            self.o(dz, me.z, 1).wait_send()
        for dz in range(1, 4):
            self.m(dz).wait_send()


def pick_piece(kind, x, y, z, zsrc):
    every = slice(None)
    if kind == "q":
        return (y, x % 2, zsrc // 2, x // 2, every, lanes_of(z))
    return (y, x // 2, zsrc // 2, x % 2, every, lanes_of(z))


class Collect:
    def __init__(self, me, oq, oo, om, finals, send, recv, local):
        self.me, self.oq, self.oo, self.om, self.finals = me, oq, oo, om, finals
        self.send, self.recv, self.local = send, recv, local

    def qk(self, kind, dz):
        me = self.me
        own, col = mapping(me, kind)
        z = (me.z + dz) % 4
        keep = (own == 1) if dz == 0 else None
        return Route(keep, self.finals[kind].at[z // 2], self.oq.at[:, lanes_of(me.z)], self.send.at[dz],
                     self.recv.at[dz], self.local.at[0], me.dev(z=z, **col))

    def o(self, dz):
        me = self.me
        own, col = mapping(me, "o")
        z = (me.z + dz) % 4
        keep = (own == 1) if dz == 0 else None
        return Route(keep, self.finals["o"].at[z % 2, z // 2], self.oo.at[:, lanes_of(me.z)], self.send.at[4 + dz],
                     self.recv.at[4 + dz], self.local.at[1], me.dev(z=z, **col))

    def m(self, t, kind, dz):
        me = self.me
        z = (me.z + dz) % 4
        n = 8 + 4 * t + dz
        src = self.finals[kind].at[z // 2, pl.ds(pl.multiple_of((z % 2) * 24, 8), 24)]
        dst = self.om.at[pl.ds(t * 24, 24), lanes_of(me.z)]
        if dz == 0:
            return pltpu.make_async_copy(src, dst, self.local.at[2 + t])
        return remote(src, dst, self.send.at[n], self.recv.at[n], me.dev(z=z))

    def each_qk(self, act):
        me = self.me
        for dz in range(4):
            for kind, low in (("q", 0), ("k", 1)):
                @pl.when((me.z + dz) % 2 == low)
                def _(kind=kind, dz=dz):
                    act(self.qk(kind, dz))

    def start(self, kind):
        if kind == "qk":
            self.each_qk(lambda r: r.start())
        elif kind == "o":
            for dz in range(4):
                self.o(dz).start()
        else:
            for dz in range(4):
                self.m("gud".index(kind), kind, dz).start()

    def finish(self, kind):
        me = self.me
        if kind == "qk":
            for dz in range(4):
                for k, low in (("q", 0), ("k", 1)):
                    @pl.when(me.zlo == low)
                    def _(k=k, dz=dz):
                        self.qk(k, dz).wait_recv()
            self.each_qk(lambda r: r.wait_send())
        elif kind == "o":
            for dz in range(4):
                self.o(dz).wait_recv()
                self.o(dz).wait_send()
        else:
            for dz in range(4):
                c = self.m("gud".index(kind), kind, dz)
                if dz == 0:
                    c.wait()
                else:
                    c.wait_recv()
                    c.wait_send()


def dot(a, b):
    return jnp.dot(a, b, preferred_element_type=F32)


def dot_t(a, b):
    return lax.dot_general(a, b, (((1,), (1,)), ((), ())), preferred_element_type=F32)


def dot_c(a, b):
    return lax.dot_general(a, b, (((0,), (0,)), ((), ())), preferred_element_type=F32)


def mean_last(v):
    return jnp.mean(v, axis=-1, keepdims=True)


def norm_scale(v):
    return lax.rsqrt(mean_last(v * v) + EPSILON)


def norm_back(dz, v, gain):
    r = norm_scale(v)
    n = v * r
    w = dz * gain
    return r * (w - n * mean_last(w * n)), dz * n


def fold_rows(v):
    return jnp.sum(v.reshape(v.shape[0] // 8, 8, v.shape[1]), axis=0)


def rows_of(i, n):
    return pl.ds(pl.multiple_of(i * n, n), n)


class SmallSum:
    def __init__(self, me, buf, land, send, recv):
        self.me, self.buf, self.land, self.send, self.recv = me, buf, land, send, recv

    def copies(self, stage):
        if stage == 0:
            return [remote(self.buf, self.land.at[0], self.send.at[0], self.recv.at[0], self.me.dev(core=1 - self.me.core))]
        first = 1 + 3 * (stage - 1)
        return [remote(self.buf, self.land.at[first + s], self.send.at[stage], self.recv.at[stage],
                       self.me.ring("xyz"[stage - 1], s + 1)) for s in range(3)]

    def start(self, stage):
        for c in self.copies(stage):
            c.start()

    def finish(self, stage):
        if stage == 0:
            self.copies(0)[0].wait()
            self.buf[...] = self.buf[...] + self.land[0]
        else:
            first = 1 + 3 * (stage - 1)
            three = self.land.at[pl.ds(first, 3)]
            remote(three, three, self.send.at[stage], self.recv.at[stage], self.me.ring("xyz"[stage - 1], 1)).wait()
            self.buf[...] = self.buf[...] + (self.land[first] + self.land[first + 1] + self.land[first + 2])


class Layer:
    def __init__(self, me, S):
        self.me = me
        self.__dict__.update(S)
        c = me.core
        self.mine = rows_of(c, 256)
        self.theirs = rows_of(1 - c, 256)
        self.peer = me.dev(core=1 - c)
        self.wq2 = self.bq.reshape(1024, 1024)
        self.wk2 = self.bk.reshape(1024, 1024)
        self.wo2 = self.bo.reshape(1024, 1024)
        self.mlp = [[S["b" + k].at[j].reshape(768, 1024) for k in "gud"] for j in range(2)]
        self.dq2 = self.tq.reshape(1024, 1024)
        self.dk2 = self.tk.reshape(1024, 1024)
        self.cx, self.mi = self.dq2.at[pl.ds(0, 512)], self.dq2.at[pl.ds(512, 512)]
        self.es = self.dp.at[:, pl.ds(0, 1024)]
        self.lob, self.igb = self.ct.at[pl.ds(0, 256)], self.ct.at[pl.ds(256, 256)]
        self.da, self.dc = self.dk2.at[pl.ds(0, 512)], self.dk2.at[pl.ds(512, 512)]

    def swap(self, n, src, dst):
        me = self.me
        return Route(me.core == me.zlo, src, dst, self.xsend.at[n], self.xrecv.at[n], self.xlocal.at[n],
                     me.dev(z=me.zhi * 2 + me.core, core=me.zlo))

    def share(self, n, src, dst):
        return remote(src, dst, self.xsend.at[n], self.xrecv.at[n], self.peer)

    def tokens_in(self):
        there = self.me.zlo
        return [self.swap(0, self.x_in, self.xa.at[rows_of(there, 256)]),
                self.swap(1, self.seg_in, self.seg.at[there]),
                self.swap(2, self.pos_in, self.pos.at[there]),
                self.swap(3, self.ct_in, self.ct.at[rows_of(there, 256)])]

    def send_piece(self, n, i):
        src, dst = (self.x_in, self.xa) if n == 0 else (self.ct_in, self.ct)
        self.swap(n, src.at[pl.ds(i * 64, 64)], dst.at[pl.ds(pl.multiple_of(self.me.zlo * 256 + i * 64, 64), 64)]).start()

    def tokens_across(self):
        m = self.mine
        c = self.me.core
        return [self.share(4, self.xa.at[m], self.xa.at[m]),
                self.share(5, self.seg.at[c], self.seg.at[c]),
                self.share(6, self.pos.at[c], self.pos.at[c]),
                self.share(7, self.ct.at[m], self.ct.at[m])]

    def gains_rows(self):
        for i in range(8):
            cols = slice(i * 128, (i + 1) * 128)
            self.gv[0:1, cols] = self.ga[i:i + 1, :]
            self.gv[1:2, cols] = self.ga[8 + i:9 + i, :]
        self.gv[2:3, 0:128] = self.ga[16:17, :]
        self.gv[2:3, 128:256] = self.ga[17:18, :]

    def tables(self):
        lane = lax.broadcasted_iota(jnp.int32, (1, 128), 1)
        freqs = jnp.exp((lane % 64).astype(F32) * (-2.0 * math.log(THETA_BASE) / HEAD))
        sign = jnp.where(lane < 64, -1.0, 1.0)
        for h in range(2):
            angle = jnp.broadcast_to(self.pos[h].astype(F32), (128, 256)).T * freqs
            self.cosine[h * 256:(h + 1) * 256] = jnp.cos(angle)
            self.sine[h * 256:(h + 1) * 256] = jnp.sin(angle) * sign
        for q in range(2):
            seg_q = self.seg[q].astype(F32)
            for k in range(q + 1):
                seg_k = jnp.broadcast_to(self.seg[k].astype(F32), (128, 256)).T[:, 0:1]
                key = lax.broadcasted_iota(jnp.int32, (256, 256), 0) + k * 256
                query = lax.broadcasted_iota(jnp.int32, (256, 256), 1) + q * 256
                allowed = (seg_q == seg_k) & (key <= query)
                self.mask[k * 256:(k + 1) * 256, q * 256:(q + 1) * 256] = jnp.where(allowed, 0.0, MASKED).astype(BF)

    def norm_in(self):
        gain = self.gv[0:1, :]

        @pl.loop(0, 8)
        def _(i):
            r = rows_of(i, 64)
            v = self.xa[r].astype(F32)
            self.xn[r] = (v * norm_scale(v) * gain).astype(BF)

    def rope(self, n):
        return n * self.cosine[...] + pltpu.roll(n, 64, 1) * self.sine[...]

    def unrope(self, d, rows):
        return d * self.cosine[rows] - pltpu.roll(d, 64, 1) * self.sine[rows]

    def project(self):
        gq, gk = self.gv[2:3, 0:128], self.gv[2:3, 128:256]

        @pl.loop(0, 4)
        def _(i):
            pre = dot_t(self.xn[...], self.wq2[rows_of(i, 256)])
            for g in range(2):
                v = pre[:, g * 128:(g + 1) * 128]
                cols = pl.ds(pl.multiple_of(i * 256 + g * 128, 128), 128)
                self.qp[:, cols] = v.astype(BF)
                self.qr[:, cols] = self.rope(v * norm_scale(v) * gq).astype(BF)

        @pl.loop(0, 2)
        def _(i):
            pre = dot_t(self.xn[...], self.wk2[rows_of(i, 256)])
            for g in range(2):
                v = pre[:, g * 128:(g + 1) * 128]
                cols = pl.ds(pl.multiple_of(i * 256 + g * 128, 128), 128)
                self.kp[:, cols] = v.astype(BF)
                self.kr[:, cols] = self.rope(v * norm_scale(v) * gk).astype(BF)
            self.vl[:, rows_of(i, 256)] = dot_t(self.xn[...], self.wk2[rows_of(i + 2, 256)]).astype(BF)

    def attend(self):
        factor = HEAD ** -0.5 * 1.4426950408889634

        @pl.loop(0, 4)
        def _(k):
            kcols = rows_of(k, 128)
            for b in range(2):
                n = 256 * (b + 1)
                rows = slice(b * 256, (b + 1) * 256)
                keys, values = self.kr[0:n, kcols], self.vl[0:n, kcols]
                for g in range(2):
                    qcols = pl.ds(pl.multiple_of(k * 256 + g * 128, 128), 128)
                    s = dot_t(keys, self.qr[rows, qcols])
                    p = jnp.exp2(s * factor + self.mask[0:n, rows].astype(F32))
                    p = (p * (1.0 / jnp.sum(p, axis=0, keepdims=True))).astype(BF)
                    (self.p0 if b == 0 else self.p1)[2 * k + g] = p
                    self.cx[rows, qcols] = dot_c(values, p).T.astype(BF)

    def exchange(self, n, chunk, land):
        cols = slice(chunk * 256, (chunk + 1) * 256)
        return self.share(n + chunk, self.es.at[:, cols], land.at[:, cols])

    def out_project(self):
        for j in range(4):
            cols = slice(j * 256, (j + 1) * 256)
            part = dot(self.cx[...], self.wo2[:, cols])
            self.es[:, cols] = part.astype(BF)
            self.exchange(8, j, self.r0).start()
            self.hid[:, cols] = part + self.xa[:, cols].astype(F32)

    def norm_mid(self):
        for j in range(4):
            self.exchange(8, j, self.r0).wait()
        gain = self.gv[1:2, :]

        @pl.loop(0, 8)
        def _(i):
            r = rows_of(i, 64)
            v = self.hid[r] + self.r0[r].astype(F32)
            self.hid[r] = v
            self.mi[r] = (v * norm_scale(v) * gain).astype(BF)

    def units(self, j, c):
        wg2, wu2, wd2 = self.mlp[j]
        r = rows_of(c, 256)
        gate = dot_t(self.mi[...], wg2[r])
        up = dot_t(self.mi[...], wu2[r])
        back = dot_t(self.ct[...], wd2[r])
        sig = jax.nn.sigmoid(gate)
        silu = gate * sig
        act = (silu * up).astype(BF)
        d_gate = (back * up * sig * (1.0 + gate * (1.0 - sig))).astype(BF)
        d_up = (back * silu).astype(BF)
        self.acc_d[...] += dot(d_gate, wg2[r]) + dot(d_up, wu2[r])
        return act, d_gate, d_up

    def unit_grads(self, j, c, act, d_gate, d_up):
        wg2, wu2, wd2 = self.mlp[j]
        r = rows_of(c, 256)
        self.acc_o[...] += dot(act, wd2[r])
        wd2[r] = dot_c(act, self.ct[...]).astype(BF)
        wg2[r] = dot_c(d_gate, self.mi[...]).astype(BF)
        wu2[r] = dot_c(d_up, self.mi[...]).astype(BF)

    def held_units(self, c):
        cols = rows_of(c, 256)
        upper = pl.ds(pl.multiple_of(1024 + c * 256, 256), 256)
        return self.da.at[:, cols], self.dc.at[:, cols], self.dp.at[:, upper]

    def feed_forward(self, j, c):
        self.unit_grads(j, c, *self.units(j, c))

    def feed_forward_first(self, c):
        for ref, v in zip(self.held_units(c), self.units(1, c)):
            ref[...] = v

    def feed_forward_rest(self, c):
        self.unit_grads(1, c, *(ref[...] for ref in self.held_units(c)))

    def send_mid(self):
        for j in range(4):
            cols = slice(j * 256, (j + 1) * 256)
            self.es[:, cols] = self.acc_d[:, cols].astype(BF)
            self.exchange(12, j, self.r1).start()

    def norm_mid_back(self):
        for j in range(4):
            self.exchange(12, j, self.r1).wait()
        gain = self.gv[1:2, :]

        def body(i, total):
            r = rows_of(i, 64)
            dz = self.acc_d[r] + self.r1[r].astype(F32)
            dv, term = norm_back(dz, self.hid[r], gain)
            d = self.ct[r].astype(F32) + dv
            self.acc_d[r] = d
            self.da[r] = d.astype(BF)
            return total + fold_rows(term) * (i // 4 == self.me.core).astype(F32)

        total = lax.fori_loop(0, 8, body, jnp.zeros((8, 1024), F32))
        self.gg[1:2, :] = jnp.sum(total, axis=0, keepdims=True)

    def send_output(self):
        self.ls[...] = self.acc_o[self.theirs].astype(BF)
        self.share(16, self.ls, self.r0.at[pl.ds(0, 256)]).start()

    def finish_output(self):
        self.share(16, self.ls, self.r0.at[pl.ds(0, 256)]).wait()
        self.lob[...] = (self.acc_o[self.mine] + self.hid[self.mine] + self.r0[0:256].astype(F32)).astype(BF)

    def out_back(self):
        for j in range(4):
            r = slice(j * 256, (j + 1) * 256)
            self.dc[:, r] = dot_t(self.da[...], self.wo2[r]).astype(BF)

    def attend_back(self, between):
        scale = HEAD ** -0.5
        gq, gk = self.gv[2:3, 0:128], self.gv[2:3, 128:256]

        def body(k, totals):
            total_q, total_k = totals
            r = rows_of(k, 256)
            self.wo2[r] = dot_c(self.cx[:, r], self.da[...]).astype(BF)
            kcols = rows_of(k, 128)
            dk, dv = [0.0, 0.0], [0.0, 0.0]
            for b in range(2):
                n = 256 * (b + 1)
                rows = slice(b * 256, (b + 1) * 256)
                keys, values = self.kr[0:n, kcols], self.vl[0:n, kcols]
                for g in range(2):
                    qcols = pl.ds(pl.multiple_of(k * 256 + g * 128, 128), 128)
                    low = (self.p0 if b == 0 else self.p1)[2 * k + g]
                    dc = self.dc[rows, qcols]
                    p = low.astype(F32)
                    t = p * dot_t(values, dc)
                    ds = (t - p * jnp.sum(t, axis=0, keepdims=True)).astype(BF)
                    dz = self.unrope(dot_c(keys, ds).T * scale, rows)
                    dq, term = norm_back(dz, self.qp[rows, qcols].astype(F32), gq)
                    self.dp[rows, qcols] = dq.astype(BF)
                    total_q = total_q + fold_rows(term)
                    pk, pv = dot(ds, self.qr[rows, qcols]), dot(low, dc)
                    for j in range(b + 1):
                        part = slice(j * 256, (j + 1) * 256)
                        dk[j] = dk[j] + pk[part]
                        dv[j] = dv[j] + pv[part]
            for j in range(2):
                rows = slice(j * 256, (j + 1) * 256)
                dz = self.unrope(dk[j] * scale, rows)
                dkey, term = norm_back(dz, self.kp[rows, kcols].astype(F32), gk)
                self.dp[rows, pl.ds(pl.multiple_of(1024 + k * 128, 128), 128)] = dkey.astype(BF)
                self.dp[rows, pl.ds(pl.multiple_of(1536 + k * 128, 128), 128)] = dv[j].astype(BF)
                total_k = total_k + fold_rows(term)
            between(k)
            return total_q, total_k

        zero = jnp.zeros((8, 128), F32)
        total_q, total_k = lax.fori_loop(0, 4, body, (zero, zero))
        self.gg[2:3, 0:128] = jnp.sum(total_q, axis=0, keepdims=True)
        self.gg[2:3, 128:256] = jnp.sum(total_k, axis=0, keepdims=True)

    def project_back(self, kind):
        grad, first = (self.dq2, 0) if kind == "q" else (self.dk2, 1024)

        @pl.loop(0, 4)
        def _(j):
            cols = pl.ds(pl.multiple_of(first + j * 256, 256), 256)
            grad[rows_of(j, 256)] = dot_c(self.dp[:, cols], self.xn[...]).astype(BF)

    def d_normed(self, rows):
        return dot(self.dp[rows, 0:1024], self.wq2[...]) + dot(self.dp[rows, 1024:2048], self.wk2[...])

    def send_in(self):
        self.ls[...] = self.d_normed(self.theirs).astype(BF)
        self.share(18, self.ls, self.r0.at[pl.ds(256, 256)]).start()

    def finish_input(self):
        self.hid[0:256] = self.d_normed(self.mine)
        self.share(18, self.ls, self.r0.at[pl.ds(256, 256)]).wait()
        gain = self.gv[0:1, :]

        def body(i, total):
            r = rows_of(i, 64)
            at = pl.ds(pl.multiple_of(self.me.core * 256 + i * 64, 64), 64)
            over = pl.ds(pl.multiple_of(256 + i * 64, 64), 64)
            dz = self.hid[r] + self.r0[over].astype(F32)
            dv, term = norm_back(dz, self.xa[at].astype(F32), gain)
            self.igb[r] = (self.acc_d[at] + dv).astype(BF)
            return total + fold_rows(term)

        total = lax.fori_loop(0, 4, body, jnp.zeros((8, 1024), F32))
        self.gg[0:1, :] = jnp.sum(total, axis=0, keepdims=True)

    def gains_flat(self):
        for i in range(8):
            cols = slice(i * 128, (i + 1) * 128)
            self.gs[i:i + 1, :] = self.gg[0:1, cols]
            self.gs[8 + i:9 + i, :] = self.gg[1:2, cols]
        self.gs[16:17, :] = self.gg[2:3, 0:128]
        self.gs[17:18, :] = self.gg[2:3, 128:256]
        self.gs[18:24, :] = jnp.zeros((6, 128), F32)


INPUTS = ("x_in", "ct_in", "seg_in", "pos_in", "wq_in", "wo_in", "wm_in", "gain_in")
OUTPUTS = ("lo", "ig", "oq", "oo", "om", "gs")
V, SEM = pltpu.VMEM, pltpu.SemaphoreType.DMA


def scratch():
    s = {"b" + k: V(SHAPES[k], BF) for k in KINDS}
    s.update(tq=V(SHAPES["q"], BF), tk=V(SHAPES["k"], BF))
    s.update(stage=V((4, 72, 256), F32), wqt=V((32, 1024), BF), wov=V((16, 1024), BF), wmv=V((3, 24, 1024), BF), wmf=V((72, 1024), F32))
    s.update(xa=V((512, 1024), BF), ct=V((512, 1024), BF), seg=V((2, 1, 256), jnp.int32), pos=V((2, 1, 256), jnp.int32), xn=V((512, 1024), BF))
    s.update(qp=V((512, 1024), BF), kp=V((512, 512), BF), qr=V((512, 1024), BF), kr=V((512, 512), BF), vl=V((512, 512), BF))
    s.update(cosine=V((512, 128), F32), sine=V((512, 128), F32), mask=V((512, 512), BF))
    s.update(p0=V((8, 256, 256), BF), p1=V((8, 512, 256), BF))
    s.update(hid=V((512, 1024), F32), acc_o=V((512, 1024), F32), acc_d=V((512, 1024), F32))
    s.update(r0=V((512, 1024), BF), r1=V((512, 1024), BF))
    s.update(ls=V((256, 1024), BF))
    s.update(dp=V((512, 2048), BF))
    s.update(ga=V((24, 128), F32), gv=V((8, 1024), F32), gg=V((8, 1024), F32), land_a=V((10, 24, 128), F32), land_b=V((10, 24, 128), F32))
    for k in KINDS:
        order = ORDERS[k]
        for n, (p, chunk) in enumerate(PHASES[k]):
            s["land_%s%d" % (k, n)] = V((6,) + half_shape(k, order[:p], order[p], chunk), BF)
    for k in "qkogud":
        s["final_" + k] = V({"q": (2, 32, 256), "k": (2, 32, 256), "o": (2, 2, 16, 256)}.get(k, (2, 48, 256)), F32)
    phases = 2 * sum(len(p) for p in PHASES.values())
    for name, n in (("spread", 12), ("collect", 20), ("small_a", 4), ("small_b", 4)):
        s[name + "_send"], s[name + "_recv"] = SEM((n,)), SEM((n,))
    s.update(gather_recv=SEM((phases,)), scatter_recv=SEM((phases,)))
    s.update(spread_local=SEM((2,)), collect_local=SEM((5,)), xsend=SEM((20,)), xrecv=SEM((20,)), xlocal=SEM((20,)), drained=SEM((4 * len(KINDS),)), fetch=SEM((3,)))
    return s


def kernel(*refs):
    shapes = scratch()
    S = dict(zip(INPUTS + OUTPUTS + tuple(shapes), refs))
    me = Place()
    fetch = [pltpu.make_async_copy(S[a], S[b], S["fetch"].at[n]) for n, (a, b) in
             enumerate((("wq_in", "wqt"), ("wo_in", "wov"), ("wm_in", "wmv")))]
    for c in fetch:
        c.start()
    greet(me)
    L = Layer(me, S)
    bufs = {k: S["b" + k] for k in KINDS}
    grads = dict(bufs, q=S["tq"], k=S["tk"])
    finals = {k: S["final_" + k] for k in "qkogud"}
    sp = Spread(me, S["wqt"], S["wov"], S["wmf"], bufs, S["stage"], S["spread_send"], S["spread_recv"], S["spread_local"])
    ga = SmallSum(me, S["ga"], S["land_a"], S["small_a_send"], S["small_a_recv"])
    gb = SmallSum(me, S["gs"], S["land_b"], S["small_b_send"], S["small_b_recv"])
    C = Collect(me, S["oq"], S["oo"], S["om"], finals, S["collect_send"], S["collect_recv"], S["collect_local"])
    gathers, scatters, sent, n = {}, {}, S["drained"], 0
    measure = S["bg"].reshape(1536, 1024)
    for i, k in enumerate(KINDS):
        for j, (p, chunk) in enumerate(PHASES[k]):
            two = lambda name: (S[name].at[2 * n], S[name].at[2 * n + 1])
            gathers[k, p, chunk] = Gather(me, k, p, chunk, bufs[k], None, measure, sent.at[2 * i + (chunk == 1)], two("gather_recv"))
            scatters[k, p, chunk] = Scatter(me, k, p, chunk, grads[k], S["land_%s%d" % (k, j)], measure,
                                            sent.at[12 + 2 * i + (chunk is not None)], two("scatter_recv"), finals[k] if p == 0 else None)
            n += 1

    def drain(sem, rows):
        r = ruler(measure, rows)
        remote(r, r, sem, S["gather_recv"].at[0], me.ring("x", 1)).wait_send()

    def run(table, kinds, p, chunk, acts):
        for act in acts:
            for k in kinds:
                getattr(table[k, p, chunk], act)()

    def G(kinds, p, *acts, chunk=None):
        run(gathers, kinds, p, chunk, acts)

    def R(kinds, p, *acts, chunk=None):
        run(scatters, kinds, p, chunk, acts)

    arrive = L.tokens_in()
    across = L.tokens_across()
    fetch[0].wait()
    fetch[1].wait()
    sp.start_attention()
    arrive[1].start()
    arrive[2].start()
    L.send_piece(0, 0)
    L.send_piece(0, 1)
    first = 18 * (me.zlo * 64 + me.dp)
    wide = jnp.concatenate([S["gain_in"][...].astype(F32), jnp.zeros((1, 238), F32)], axis=1)
    wide = pltpu.roll(jnp.broadcast_to(wide, (8, 256)), first % 128, 1)[0:1]
    S["ga"][...] = jnp.zeros((24, 128), F32)
    S["ga"][pl.ds(first // 128, 1), :] = wide[:, 0:128]
    S["ga"][pl.ds(first // 128 + 1, 1), :] = wide[:, 128:256]
    ga.start(0)
    fetch[2].wait()
    for t in range(3):
        S["wmf"][t * 24:(t + 1) * 24, :] = S["wmv"][t].astype(F32)
    sp.wait_attention()
    G(ATT, 0, "start")
    sp.start_mlp()
    ga.finish(0)
    ga.start(1)
    L.send_piece(0, 2)
    L.send_piece(0, 3)
    sp.wait_mlp()
    G(MLP, 0, "start")
    G(ATT, 0, "finish")
    G(ATT, 1, "start")
    L.send_piece(3, 0)
    ga.finish(1)
    ga.start(2)
    L.acc_o[...] = jnp.zeros((512, 1024), F32)
    L.acc_d[...] = jnp.zeros((512, 1024), F32)
    G(MLP, 0, "finish")
    G(MLP, 1, "start")
    G(ATT, 1, "forward")
    ga.finish(2)
    ga.start(3)
    for c in arrive[:3]:
        c.wait_recv()
    for c in across[:3]:
        c.start()
    G(ATT, 1, "finish")
    G(ATT, 2, "start")
    G(MLP, 1, "forward")
    ga.finish(3)
    L.gains_rows()
    for c in across[:3]:
        c.wait()
    L.tables()
    L.norm_in()
    G(ATT, 2, "forward")
    G(MLP, 1, "finish")
    G(MLP, 2, "start", chunk=0)
    for i in range(1, 4):
        L.send_piece(3, i)
    G(MLP, 2, "start", chunk=1)
    G(ATT, 2, "finish")
    L.project()
    G(MLP, 2, "forward", chunk=0)
    L.attend()
    arrive[3].wait_recv()
    across[3].start()
    L.out_project()
    across[3].wait()
    for c in arrive:
        c.wait_send()
    sp.drain()
    L.norm_mid()
    G(MLP, 2, "finish", chunk=0)
    for i, k in enumerate(KINDS):
        drain(sent.at[2 * i], 63 * 16 if k in ATT else 3 * 24 + 12 * 24 + 48 * 12)

    @pl.loop(0, 3)
    def _(c):
        L.feed_forward(0, c)

        @pl.when(c == 0)
        def _():
            G(MLP, 2, "forward", chunk=1)

    R(MLP, 2, "start", chunk=0)
    G(MLP, 2, "finish", chunk=1)
    for i in range(3, 6):
        drain(sent.at[2 * i + 1], 48 * 12)

    @pl.loop(0, 3)
    def _(c):
        L.feed_forward_first(c)

    L.send_mid()
    R(MLP, 2, "forward", chunk=0)
    pl.loop(0, 3)(L.feed_forward_rest)
    R(MLP, 2, "start", chunk=1)
    L.norm_mid_back()
    L.send_output()
    R(MLP, 2, "finish", chunk=0)
    L.out_back()
    R(MLP, 2, "forward", chunk=1)

    def between(k):
        @pl.when(k == 0)
        def _():
            L.finish_output()
            L.swap(17, L.lob, L.lo).start()

        @pl.when(k == 2)
        def _():
            R(MLP, 2, "finish", chunk=1)
            R(MLP, 1, "start")

    L.attend_back(between)
    R("o", 2, "start")
    L.project_back("q")
    R("q", 2, "start")
    R(MLP, 1, "forward")
    L.project_back("k")
    R("k", 2, "start")
    L.send_in()
    R("o", 2, "forward")
    R("q", 2, "forward")
    R("k", 2, "forward")
    L.finish_input()
    L.gains_flat()
    gb.start(0)
    R(MLP, 1, "finish")
    R(MLP, 0, "start")
    gb.finish(0)
    gb.start(1)
    R("o", 2, "finish")
    R("o", 1, "start")
    R("q", 2, "finish")
    R("q", 1, "start")
    R("k", 2, "finish")
    R("k", 1, "start")
    R(MLP, 0, "finish")
    for k in MLP:
        C.start(k)
    gb.finish(1)
    gb.start(2)
    R("o", 1, "forward")
    R("q", 1, "forward")
    R("k", 1, "forward")
    gb.finish(2)
    gb.start(3)
    R("o", 1, "finish")
    R("o", 0, "start")
    R("q", 1, "finish")
    R("q", 0, "start")
    R("k", 1, "finish")
    R("k", 0, "start")
    L.swap(19, L.igb, L.ig).start()
    R("o", 0, "finish")
    C.start("o")
    R("qk", 0, "finish")
    C.start("qk")
    gb.finish(3)
    for k in ("g", "u", "d", "o", "qk"):
        C.finish(k)
    for i, k in enumerate(KINDS):
        if k in ATT:
            drain(sent.at[12 + 2 * i], 63 * 16)
        else:
            drain(sent.at[12 + 2 * i], 15 * 24)
            drain(sent.at[13 + 2 * i], 96 * 12)
    for n, src, dst in ((17, L.lob, L.lo), (19, L.igb, L.ig)):
        c = L.swap(n, src, dst)
        c.wait_recv()
        c.wait_send()


def finish_kernel(*refs):
    given, gs, outs, gain_out, held, sem = refs[:5], refs[5], refs[6:11], refs[11], refs[12:17], refs[17]
    loads = [pltpu.make_async_copy(a, b, sem.at[n]) for n, (a, b) in enumerate(zip(given, held))]
    stores = [pltpu.make_async_copy(a, b, sem.at[5 + n]) for n, (a, b) in enumerate(zip(held, outs))]
    for m in loads:
        m.start()
    first = 18 * (lax.axis_index("seq") * 64 + lax.axis_index("dp"))
    wide = jnp.concatenate([gs[pl.ds(first // 128, 1), :], gs[pl.ds(first // 128 + 1, 1), :]], axis=1)
    wide = pltpu.roll(jnp.broadcast_to(wide, (8, 256)), 256 - first % 128, 1)
    gain_out[...] = wide[0:1, 0:18]
    for load, store in zip(loads, stores):
        load.wait()
        store.start()
    for m in stores:
        m.wait()


def shards(layer_input, segments, positions, qkv_weight, out_weight, mlp_weight, gains, cotangent):
    vm, hbm = pl.BlockSpec(memory_space=pltpu.VMEM), pl.BlockSpec(memory_space=pl.ANY)
    shape = jax.ShapeDtypeStruct
    lo, ig, oq, oo, om, gs = pl.pallas_call(
        kernel,
        out_shape=(shape((256, 1024), BF), shape((256, 1024), BF), shape((32, 1024), F32), shape((16, 1024), F32),
                   shape((72, 1024), F32), shape((24, 128), F32)),
        in_specs=[hbm] * 7 + [vm],
        out_specs=(hbm,) * 5 + (vm,),
        scratch_shapes=list(scratch().values()),
        compiler_params=pltpu.CompilerParams(collective_id=0, has_side_effects=True, vmem_limit_bytes=VMEM_BYTES),
    )(layer_input[0], cotangent[0], segments, positions, qkv_weight.T, out_weight, jnp.transpose(mlp_weight, (1, 0, 2)), gains.reshape(1, 18))
    lo, ig, oq, oo, om, gs = pl.pallas_call(
        finish_kernel,
        out_shape=(shape((256, 1024), BF), shape((256, 1024), BF), shape((32, 1024), F32), shape((16, 1024), F32),
                   shape((72, 1024), F32), shape((1, 18), F32)),
        in_specs=[hbm] * 5 + [vm],
        out_specs=(hbm,) * 5 + (vm,),
        scratch_shapes=[V((256, 1024), BF), V((256, 1024), BF), V((32, 1024), F32), V((16, 1024), F32), V((72, 1024), F32), SEM((10,))],
    )(lo, ig, oq, oo, om, gs)
    return lo[None], ig[None], oq.T, oo, jnp.transpose(om.reshape(3, 24, 1024), (1, 0, 2)), gs.reshape(18)


def solution(mesh):
    rows, split = P("dp", "seq", None), ("seq", "dp")
    weights = (P(None, split), P(split, None), P(split, None, None), P(split))
    return jax.shard_map(shards, mesh=mesh, in_specs=(rows, P("dp", "seq"), P("dp", "seq")) + weights + (rows,),
                         out_specs=(rows, rows) + weights, check_vma=False)
```
